32 devices in a mesh: loop: 16 (over z, x, core), tensor: 2 (over y).
Axes of the slice: x: 2, y: 2, z: 4, core: 2. Of those that a mesh axis runs over, the one named last changes fastest.
Arguments:
- grad_out: bfloat16 [2048, 4096], P('loop', 'tensor'), may hold values from -6 to 6
- saved_hidden: bfloat16 [416, 32768], P('tensor', 'loop'), may hold values from -6 to 6
- picked_tokens: int32 [2, 416], replicated, may hold values from 0 to 2047, as said below
- gate_values: float32 [2, 416], replicated, may hold values from 0.25 to 1
- in_weight: bfloat16 [4096, 32768], P(None, 'loop'), may hold values from -0.09375 to 0.09375
- out_weight: bfloat16 [32768, 4096], P('loop'), may hold values from -0.046875 to 0.046875
Outputs:
- input_grad: bfloat16 [2048, 4096], P('loop', 'tensor')
The draws below stay inside these ranges and needn't reach their ends.
Inputs may be any that keep to these rules, and one draw needn't show every extreme that they name: Each row picked_tokens[e] lists 416 distinct token indices in ascending order; among the 128 tokens of one loop index (an aligned block) it names at most 28, and in every row some block holds exactly 28.
All inputs are finite; a program needn't handle non-finite values.
Results may differ from the reference program's by a relative error of at most 0.0032.
Values may be sent and summed in bfloat16 or wider, within the bound.
No kernel may reach another device: no remote copies, remote signals or barrier semaphores. Data moves between devices by JAX's collectives and lax.ppermute only.
A program may use at most 128 MiB of HBM per device.

```python
import math
import jax
import jax.numpy as jnp

D = 4096
FF = 16384
EXPERTS = 2
PB = 26
SWING = 2
TOK_LOOP = 128
CAP = 416
TOKENS = 2048


def shuffle_block(block_key):
    return jax.random.permutation(block_key, TOK_LOOP)


def draw_picked_tokens(key, part):
    block_total = TOKENS // TOK_LOOP
    expert_keys = jax.random.split(jax.random.fold_in(key, 7), EXPERTS)

    def one_expert(subkey):
        quota_key, order_key = jax.random.split(subkey)
        shuffled = jax.random.permutation(quota_key, block_total)
        pair_count = block_total // 4
        raised = shuffled[0:2 * pair_count:2]
        lowered = shuffled[1:2 * pair_count:2]
        quotas = jnp.full((block_total,), PB, jnp.int32).at[raised].add(SWING).at[lowered].add(-SWING)
        order_keys = jax.random.split(order_key, block_total)
        shuffles = jax.vmap(shuffle_block)(order_keys)
        ranking = jnp.argsort(shuffles, axis=1).astype(jnp.int32)
        chosen = ranking < quotas[:, None]
        return jnp.nonzero(chosen.reshape(-1), size=CAP)[0].astype(jnp.int32)
    return jax.vmap(one_expert)(expert_keys)


def block_levels(stream_key, shape, cuts, smallest, largest):
    gain = 1.0
    for axis_at, blocks in cuts:
        draws = jax.random.uniform(jax.random.fold_in(jax.random.fold_in(stream_key, 6), axis_at), (blocks,), jnp.float32, smallest / len(cuts), largest / len(cuts))
        gain = gain * jnp.repeat(jnp.exp(draws), shape[axis_at] // blocks).reshape((-1,) + (1,) * (len(shape) - 1 - axis_at))
    return gain


def noise(stream_key, dims, spread, reach, cuts=(), kind=jnp.bfloat16):
    values = jax.random.normal(stream_key, dims, jnp.float32) * spread
    if len(cuts) > 0:
        values = block_levels(stream_key, dims, cuts, -0.22, 0.18) * values
    return jnp.clip(values, min=-reach, max=reach).astype(kind)


def setup_inputs(seed: int = 0) -> dict:
    keys = jax.random.split(jax.random.key(seed), 7)
    grad_out = noise(keys[0], (TOKENS, D), 1.0, 6.0, ((0, 16), (1, 2)))
    saved_hidden = noise(keys[1], (CAP, EXPERTS * FF), 1.5, 6.0, ((0, 2), (1, 16)))
    picked_tokens = draw_picked_tokens(jax.random.fold_in(keys[6], 71), 0)
    gate_values = jnp.clip(jax.random.uniform(keys[3], (EXPERTS, CAP), jnp.float32, 0.25, 1.0), 0.25, 1.0)
    in_weight = noise(keys[4], (D, EXPERTS * FF), D ** -0.5, 0.09375, ((1, 16),))
    out_weight = noise(keys[5], (EXPERTS * FF, D), FF ** -0.5, 0.046875, ((0, 16),))
    return {"grad_out": grad_out, "saved_hidden": saved_hidden, "picked_tokens": picked_tokens, "gate_values": gate_values, "in_weight": in_weight, "out_weight": out_weight}


slope_scale = math.sqrt(2.0 / math.pi)

def gelu_slope(values):
    inner = slope_scale * (values + 0.044715 * values * values * values)
    bent = jnp.tanh(inner)
    return 0.5 * (1.0 + bent) + 0.5 * values * (1.0 - bent * bent) * slope_scale * (1.0 + 0.134145 * values * values)

def reference(grad_out, saved_hidden, picked_tokens, gate_values, in_weight, out_weight):
    moe_grad = jnp.zeros((TOKENS, D), jnp.float32)
    for expert in range(EXPERTS):
        chosen = picked_tokens[expert]
        scaled = (gate_values[expert][:, None] * grad_out[chosen].astype(jnp.float32)).astype(jnp.bfloat16)
        out_block = out_weight[expert * FF:(expert + 1) * FF]
        act_grad = jnp.dot(scaled, out_block.T, preferred_element_type=jnp.float32)
        hidden_block = saved_hidden[:, expert * FF:(expert + 1) * FF].astype(jnp.float32)
        pre_grad = (act_grad * gelu_slope(hidden_block)).astype(jnp.bfloat16)
        in_block = in_weight[:, expert * FF:(expert + 1) * FF]
        partial_grad = jnp.dot(pre_grad, in_block.T, preferred_element_type=jnp.float32)
        moe_grad = moe_grad.at[chosen].add(partial_grad)
    return (grad_out.astype(jnp.float32) + moe_grad).astype(jnp.bfloat16)
```

```python
import math

import jax
import jax.numpy as jnp
from jax import lax
from jax.sharding import PartitionSpec as P

MOST = 28
BOTH = ("loop", "tensor")

slope_scale = math.sqrt(2.0 / math.pi)


def gelu_slope(values):
    inner = slope_scale * (values + 0.044715 * values * values * values)
    bent = jnp.tanh(inner)
    return 0.5 * (1.0 + bent) + 0.5 * values * (1.0 - bent * bent) * slope_scale * (
        1.0 + 0.134145 * values * values
    )


def rows_dot(left, right, out_type=jnp.float32):
    return lax.dot_general(
        left, right, (((1,), (1,)), ((), ())), preferred_element_type=jnp.float32
    ).astype(out_type)


def swap(values, distance):
    pairs = [(source, source ^ distance) for source in range(lax.axis_size("loop"))]
    return lax.ppermute(values, "loop", pairs)


def home_routes(expert_count):
    loop_size, tensor_size = lax.axis_size("loop"), lax.axis_size("tensor")
    blocks = loop_size // tensor_size
    group_size = loop_size // expert_count
    splits = group_size // blocks
    routes = []
    for turn in range(expert_count):
        pairs = []
        for loop_at in range(loop_size):
            for tensor_at in range(tensor_size):
                expert = (tensor_at + turn) % expert_count
                place = (loop_at % blocks) * splits + tensor_at // expert_count
                target = (expert * group_size + place) * tensor_size + loop_at // blocks
                pairs.append((loop_at * tensor_size + tensor_at, target))
        routes.append(pairs)
    return routes


def widen_rows(saved, halo):
    row_count = saved.shape[0]
    size = lax.axis_size("tensor")
    before, after = [], []
    for hop in range(1, -(-halo // row_count) + 1):
        part = min(row_count, halo - (hop - 1) * row_count)
        up = [(at, at + hop) for at in range(size - hop)]
        before.insert(0, lax.ppermute(saved[row_count - part :], "tensor", up))
        after.append(lax.ppermute(saved[:part], "tensor", [(b, a) for a, b in up]))
    return jnp.concatenate(before + [saved] + after, axis=0)


def shards(grad_out, saved_hidden, picked_tokens, gate_values, in_weight, out_weight):
    home_rows, feature_cols = grad_out.shape
    width = in_weight.shape[0]
    loop_size, tensor_size = lax.axis_size("loop"), lax.axis_size("tensor")
    expert_count, capacity = picked_tokens.shape
    blocks = loop_size // tensor_size
    group_size = loop_size // expert_count
    splits = group_size // blocks
    loop_index, tensor_index = lax.axis_index("loop"), lax.axis_index("tensor")
    expert_id, place = loop_index // group_size, loop_index % group_size
    routes = home_routes(expert_count)

    tokens = loop_index * home_rows + jnp.arange(home_rows, dtype=jnp.int32)
    same = picked_tokens[:, None, :] == tokens[None, :, None]
    picked_here = jnp.any(same, axis=2)
    gates = jnp.sum(jnp.where(same, gate_values[:, None, :], 0.0), axis=2)
    rank = jnp.cumsum(picked_here.astype(jnp.int32), axis=1) - 1
    slots = jnp.arange(MOST, dtype=jnp.int32)
    chosen = picked_here[:, None, :] & (rank[:, None, :] == slots[None, :, None])
    chosen = chosen.astype(jnp.bfloat16)
    wide = grad_out.astype(jnp.float32)

    arrived = []
    for turn in range(expert_count):
        expert = (tensor_index + turn) % expert_count
        gate = lax.dynamic_index_in_dim(gates, expert, 0, keepdims=False)
        pick = lax.dynamic_index_in_dim(chosen, expert, 0, keepdims=False)
        scaled = (gate[:, None] * wide).astype(jnp.bfloat16)
        outgoing = jnp.dot(pick, scaled, preferred_element_type=jnp.float32)
        arrived.append(lax.ppermute(outgoing.astype(jnp.bfloat16), BOTH, routes[turn]))
    arrived = jnp.stack(arrived)
    turns = (expert_id - jnp.arange(expert_count)) % expert_count
    mine = jnp.concatenate(
        [lax.dynamic_index_in_dim(arrived, turns[s], 0, keepdims=False) for s in range(expert_count)],
        axis=1,
    )

    cross = [mine] + [swap(mine, 2 * m) for m in range(1, group_size // 2)]
    pieces = []
    for piece in cross:
        pieces += [piece, swap(piece, 1)]
    if splits > 1:
        order = (place % splits) ^ jnp.arange(splits)
        rows = jnp.stack(pieces).reshape(blocks, splits, MOST, width // splits)
        rows = jnp.take(rows, order, axis=1).swapaxes(1, 2).reshape(blocks * MOST, width)
    else:
        rows = jnp.concatenate(pieces, axis=0)

    per_tensor = capacity // tensor_size
    halo = max(
        max(MOST * cut * blocks - cut * per_tensor, cut * per_tensor - capacity + MOST * (tensor_size - cut) * blocks)
        for cut in range(1, tensor_size)
    )
    window = widen_rows(saved_hidden, halo)
    own_picks = lax.dynamic_index_in_dim(picked_tokens, expert_id, 0, keepdims=False)
    block_ids = tensor_index * blocks + ((place // splits) ^ jnp.arange(blocks, dtype=jnp.int32))
    first = jnp.sum((own_picks[None, :] < (block_ids * home_rows)[:, None]).astype(jnp.int32), axis=1)
    offsets = (first[:, None] + slots[None, :]).reshape(-1) - tensor_index * per_tensor + halo
    take = offsets[:, None] == jnp.arange(window.shape[0], dtype=jnp.int32)[None, :]
    hidden = jnp.dot(take.astype(jnp.bfloat16), window, preferred_element_type=jnp.float32)

    act_grad = rows_dot(rows, out_weight)
    pre_grad = (act_grad * gelu_slope(hidden)).astype(jnp.bfloat16)
    partial = rows_dot(pre_grad, in_weight)

    if splits > 1:
        partial = partial.reshape(blocks, MOST, splits, width // splits).swapaxes(1, 2)
        partial = jnp.take(partial, order, axis=1)
    partial = partial.reshape(group_size // 2, 2, MOST, width // splits)
    got = swap(partial[:, 1].astype(jnp.bfloat16), 1)
    paired = partial[:, 0] + got.astype(jnp.float32)
    total = paired[0]
    for m in range(1, group_size // 2):
        total = total + swap(paired[m].astype(jnp.bfloat16), 2 * m).astype(jnp.float32)
    total = total.astype(jnp.bfloat16).reshape(MOST, expert_count, feature_cols)

    summed = wide
    for turn in range(expert_count):
        sending = lax.dynamic_index_in_dim(total, turns[turn], 1, keepdims=False)
        back = [(target, source) for source, target in routes[turn]]
        landed = lax.ppermute(sending, BOTH, back)
        expert = (tensor_index + turn) % expert_count
        pick = lax.dynamic_index_in_dim(chosen, expert, 0, keepdims=False)
        summed = summed + lax.dot_general(
            pick, landed, (((0,), (0,)), ((), ())), preferred_element_type=jnp.float32
        )
    return summed.astype(jnp.bfloat16)


def solution(mesh):
    placed = (P("loop", "tensor"), P("tensor", "loop"), P(), P(), P(None, "loop"), P("loop", None))
    return jax.shard_map(
        shards, mesh=mesh, in_specs=placed, out_specs=P("loop", "tensor"), check_vma=False
    )
```

```python
import functools
import math

import jax
import jax.numpy as jnp
from jax import lax
from jax.experimental import pallas as pl
from jax.experimental.pallas import tpu as pltpu
from jax.sharding import PartitionSpec as P

MOST = 28
PADDED = 32
BOTH = ("loop", "tensor")
VMEM = pl.BlockSpec(memory_space=pltpu.VMEM)
LEFT = pl.BlockSpec(memory_space=pl.ANY)

slope_scale = math.sqrt(2.0 / math.pi)


def gelu_slope(values):
    inner = slope_scale * (values + 0.044715 * values * values * values)
    bent = jnp.tanh(inner)
    return 0.5 * (1.0 + bent) + 0.5 * values * (1.0 - bent * bent) * slope_scale * (
        1.0 + 0.134145 * values * values
    )


def rows_dot(left, right):
    return lax.dot_general(left, right, (((1,), (1,)), ((), ())), preferred_element_type=jnp.float32)


def kernel_call(body, out_shape, operands, scratch=(), flops=0, vmem=4, left=0):
    nbytes = sum(o.size * o.dtype.itemsize for o in operands)
    operands = [
        pltpu.with_memory_space_constraint(o, pltpu.HBM) if at < left else o
        for at, o in enumerate(operands)
    ]
    return pl.pallas_call(
        body,
        out_shape=out_shape,
        in_specs=[LEFT] * left + [VMEM] * (len(operands) - left),
        out_specs=jax.tree.map(lambda _: VMEM, out_shape),
        scratch_shapes=scratch,
        cost_estimate=pl.CostEstimate(flops=flops, bytes_accessed=nbytes, transcendentals=0),
        compiler_params=pltpu.CompilerParams(vmem_limit_bytes=vmem << 20),
    )(*operands)


def after_all(values, others):
    values = tuple(values)
    return lax.optimization_barrier((values, tuple(others)))[0]


def swap(values, distance):
    pairs = [(source, source ^ distance) for source in range(lax.axis_size("loop"))]
    return lax.ppermute(values, "loop", pairs)


def home_routes(expert_count):
    loop_size, tensor_size = lax.axis_size("loop"), lax.axis_size("tensor")
    blocks = loop_size // tensor_size
    group_size = loop_size // expert_count
    splits = group_size // blocks
    routes = []
    for turn in range(expert_count):
        pairs = []
        for loop_at in range(loop_size):
            for tensor_at in range(tensor_size):
                expert = (tensor_at + turn) % expert_count
                place = (loop_at % blocks) * splits + tensor_at // expert_count
                target = (expert * group_size + place) * tensor_size + loop_at // blocks
                pairs.append((loop_at * tensor_size + tensor_at, target))
        routes.append(pairs)
    return routes


def home_slots(picks, start, home_rows):
    capacity = picks.shape[1]
    first = jnp.sum((picks < start).astype(jnp.int32), axis=1, keepdims=True)
    slot = lax.broadcasted_iota(jnp.int32, (PADDED, capacity), 0)
    listed = lax.broadcasted_iota(jnp.int32, (PADDED, capacity), 1) == first + slot
    local = jnp.sum(jnp.where(listed, picks - start + 1, 0), axis=1, keepdims=True) - 1
    tokens = lax.broadcasted_iota(jnp.int32, (PADDED, home_rows), 1)
    return listed, (tokens == local).astype(jnp.bfloat16)


def prepare_kernel(grad_from, picked_from, gates_from, saved_from, *refs):
    outs, edge, (grad, picked, gates, arrived) = refs[:-5], refs[-5], refs[-4:]
    expert_count = len(outs)
    spare = saved_from.shape[0] - edge.shape[0]
    first = jnp.where(lax.axis_index("tensor") == 0, spare, 0)
    saved_rows = saved_from.at[pl.ds(pl.multiple_of(first, 16), edge.shape[0]), :]
    copies = [
        pltpu.make_async_copy(source, target, arrived.at[at])
        for at, (source, target) in enumerate(
            ((picked_from, picked), (gates_from, gates), (grad_from, grad), (saved_rows, edge))
        )
    ]
    for copy in copies:
        copy.start()
    home_rows = grad.shape[0]
    start = lax.axis_index("loop") * home_rows
    copies[0].wait()
    copies[1].wait()
    rows = []
    for turn in range(expert_count):
        expert = lax.rem(lax.axis_index("tensor") + turn, expert_count)
        listed, chosen = home_slots(picked[pl.ds(expert, 1), :], start, home_rows)
        gate = jnp.sum(jnp.where(listed, gates[pl.ds(expert, 1), :], 0.0), axis=1, keepdims=True)
        rows.append((gate, chosen))
    copies[2].wait()
    for (gate, chosen), out in zip(rows, outs):
        taken = jnp.dot(chosen, grad[...], preferred_element_type=jnp.float32)
        out[...] = (gate * taken).astype(jnp.bfloat16)[:MOST]
    copies[3].wait()


def finish_kernel(expert_count, grad, picked, *refs):
    landed, out, held = refs[:expert_count], refs[expert_count], refs[expert_count + 1]
    home_rows = grad.shape[0]
    start = lax.axis_index("loop") * home_rows
    total = grad[...].astype(jnp.float32)
    for turn in range(expert_count):
        expert = lax.rem(lax.axis_index("tensor") + turn, expert_count)
        _, chosen = home_slots(picked[pl.ds(expert, 1), :], start, home_rows)
        held[...] = jnp.zeros_like(held)
        held[:MOST, :] = landed[turn][...]
        total += lax.dot_general(
            chosen, held[...], (((0,), (0,)), ((), ())), preferred_element_type=jnp.float32
        )
    out[...] = total.astype(jnp.bfloat16)


def part_start(turn, split, splits, expert_count, group_size, features):
    loop_index = lax.axis_index("loop")
    mine = lax.rem(lax.rem(loop_index, group_size), splits) ^ split
    share = lax.rem(loop_index // group_size - turn + expert_count, expert_count)
    return pl.multiple_of((mine * expert_count + share) * features, 128)


def weight_copies(turn, sizes, axis, weight, out, arrived):
    _, splits, expert_count, group_size = sizes
    features = out.shape[1 + axis]
    parts = arrived.shape[1]
    step = out.shape[1] // parts
    copies = []
    for split in range(splits):
        start = part_start(turn, split, splits, expert_count, group_size, features)
        for at in range(parts):
            rows = pl.ds(at * step, step)
            if axis == 1:
                source = weight.at[rows, pl.ds(start, features)]
            else:
                source = weight.at[pl.ds(pl.multiple_of(start + at * step, 16), step), :]
            copies.append(pltpu.make_async_copy(source, out.at[split, rows], arrived.at[split, at]))
            copies[-1].start()
    return copies


def fetch_kernel(wanted, sizes, out_weight, in_weight, *refs):
    outs, arrived = refs[:-1], refs[-1]
    copies = []
    for at, (turn, axis) in enumerate(wanted):
        weight = out_weight if axis == 1 else in_weight
        copies += weight_copies(turn, sizes, axis, weight, outs[at], arrived.at[at])
    for copy in copies:
        copy.wait()


def slope_kernel(turns, sizes, home_rows, halo, in_weight, picked, *refs):
    blocks, splits, _, group_size = sizes
    refs, arrived = refs[:-1], refs[-1]
    refs, brought = refs[: len(refs) - len(turns)], refs[len(refs) - len(turns) :]
    parts, out = refs[:-1], refs[-1]
    copies = []
    for at, turn in enumerate(turns):
        copies += weight_copies(turn, sizes, 0, in_weight, brought[at], arrived.at[at])
    loop_index, tensor_index = lax.axis_index("loop"), lax.axis_index("tensor")
    picks = picked[pl.ds(loop_index // group_size, 1), :]
    place = lax.rem(loop_index, group_size) // splits
    per_tensor = parts[len(parts) // 2].shape[0]
    window = jnp.concatenate([part[...] for part in parts], axis=0)
    for at in range(blocks):
        block = tensor_index * blocks + (place ^ at)
        first = jnp.sum((picks < block * home_rows).astype(jnp.int32), axis=1, keepdims=True)
        wanted = first + lax.broadcasted_iota(jnp.int32, (MOST, window.shape[0]), 0)
        wanted = wanted - tensor_index * per_tensor + halo
        held = lax.broadcasted_iota(jnp.int32, (MOST, window.shape[0]), 1)
        hidden = jnp.dot(
            (held == wanted).astype(jnp.bfloat16), window, preferred_element_type=jnp.float32
        )
        out[at * MOST : (at + 1) * MOST, :] = gelu_slope(hidden)
    for copy in copies:
        copy.wait()


def join_kernel(*refs):
    for at, part in enumerate(refs[:-1]):
        refs[-1][at] = part[...]


def up_product(sizes, slope, weights, pieces, gathered, pre_grad):
    blocks, splits = sizes[:2]
    hidden = slope.shape[1]
    step = min(512, hidden)
    for turn in range(len(weights)):
        for split in range(splits):
            for at in range(blocks):
                rows = slice(at * MOST, (at + 1) * MOST)
                gathered[turn, split, rows, :] = pieces[at * splits + split][turn]
    for low in range(0, hidden, step):
        columns = slice(low, low + step)
        total = 0.0
        for turn, weight in enumerate(weights):
            for split in range(splits):
                total += rows_dot(gathered[turn, split], weight[split, columns])
        pre_grad[:, columns] = (total * slope[:, columns]).astype(jnp.bfloat16)


def down_product(sizes, pre_grad, weight, keep, give):
    blocks, splits = sizes[:2]
    features = weight.shape[1]
    step = min(512, features)
    for split in range(splits):
        for low in range(0, features, step):
            columns = slice(low, low + step)
            product = rows_dot(pre_grad[...], weight[split, columns]).astype(jnp.bfloat16)
            for at in range(blocks):
                index = at * splits + split
                target = give if index % 2 else keep
                target[index // 2, :, columns] = product[at * MOST : (at + 1) * MOST]


def both_kernel(sizes, *refs):
    expert_count = sizes[2]
    weights, down_weight, slope = refs[:expert_count], refs[expert_count], refs[expert_count + 1]
    pieces, (pre_grad, keep, give, gathered) = refs[expert_count + 2 : -4], refs[-4:]
    up_product(sizes, slope, weights, pieces, gathered, pre_grad)
    down_product(sizes, pre_grad, down_weight, keep, give)


def down_kernel(sizes, weight, pre_grad, keep, give):
    down_product(sizes, pre_grad, weight, keep, give)


def shards(grad_out, saved_hidden, picked_tokens, gate_values, in_weight, out_weight):
    home_rows, features = grad_out.shape
    width, hidden = in_weight.shape
    loop_size, tensor_size = lax.axis_size("loop"), lax.axis_size("tensor")
    expert_count, capacity = picked_tokens.shape
    blocks = loop_size // tensor_size
    group_size = loop_size // expert_count
    splits = group_size // blocks
    sizes = (blocks, splits, expert_count, group_size)
    row_count = blocks * MOST
    routes = home_routes(expert_count)
    bf16, f32 = jnp.bfloat16, jnp.float32

    order = list(range(expert_count))[::-1]
    back_order = order[::-1]
    per_tensor = capacity // tensor_size
    halo = max(
        (
            max(MOST * cut * blocks - cut * per_tensor, cut * per_tensor - capacity + MOST * (tensor_size - cut) * blocks)
            for cut in range(1, tensor_size)
        ),
        default=0,
    )
    halo = -(-halo // 16) * 16
    *outgoing, edge = kernel_call(
        prepare_kernel,
        [jax.ShapeDtypeStruct((MOST, features), bf16)] * expert_count
        + [jax.ShapeDtypeStruct((min(halo, per_tensor // 16 * 16), hidden), bf16)],
        (grad_out, picked_tokens, gate_values, saved_hidden),
        [
            pltpu.VMEM(grad_out.shape, bf16),
            pltpu.VMEM(picked_tokens.shape, jnp.int32),
            pltpu.VMEM(gate_values.shape, f32),
            pltpu.SemaphoreType.DMA((4,)),
        ],
        left=4,
    )
    arrived = {turn: lax.ppermute(outgoing[turn], BOTH, routes[turn]) for turn in order}

    parts = 4
    up_shape = pltpu.VMEM((splits, hidden, features), bf16)
    down_shape = pltpu.VMEM((splits, features, hidden), bf16)
    wanted = [(turn, 1) for turn in order] + [(back_order[0], 0)]
    sources = after_all((out_weight, in_weight), outgoing)
    fetched = kernel_call(
        functools.partial(fetch_kernel, wanted, sizes),
        [up_shape if axis == 1 else down_shape for _, axis in wanted],
        sources,
        [pltpu.SemaphoreType.DMA((len(wanted), splits, parts))],
        left=2,
    )
    arrived = after_all([arrived[turn] for turn in order], fetched)
    up_weight, down_weight = fetched[:-1], {back_order[0]: fetched[-1]}

    mine = kernel_call(join_kernel, jax.ShapeDtypeStruct((expert_count, MOST, features), bf16), arrived)
    cross = [swap(mine, 2 * m) for m in range(1, group_size // 2)]
    beside = swap(mine, 1)

    saved, edge, down_source = after_all((saved_hidden, edge, in_weight), [beside])
    before, after = [], []
    if tensor_size == 2 and halo <= per_tensor:
        before = after = [lax.ppermute(edge, "tensor", [(0, 1), (1, 0)])]
    else:
        for hop in range(1, -(-halo // per_tensor) + 1):
            part = min(per_tensor, halo - (hop - 1) * per_tensor)
            up = [(at, at + hop) for at in range(tensor_size - hop)]
            before.insert(0, lax.ppermute(saved[per_tensor - part :], "tensor", up))
            after.append(lax.ppermute(saved[:part], "tensor", [(b, a) for a, b in up]))
    slope, *fetched = kernel_call(
        functools.partial(slope_kernel, back_order[1:], sizes, home_rows, halo),
        [jax.ShapeDtypeStruct((row_count, hidden), f32)] + [down_shape] * (expert_count - 1),
        (down_source, picked_tokens, *before, saved, *after),
        [pltpu.SemaphoreType.DMA((max(1, expert_count - 1), splits, parts))],
        flops=2 * row_count * hidden * (per_tensor + 2 * halo),
        left=1,
    )
    down_weight.update(zip(back_order[1:], fetched))
    gathered = [mine, beside]
    gathered += [piece for got in after_all(cross, [slope]) for piece in (got, swap(got, 1))]

    half = 2 * row_count * hidden * features * splits
    halves = [jax.ShapeDtypeStruct((group_size // 2, MOST, features), bf16)] * 2
    made = {}
    pre_grad, *made[back_order[0]] = kernel_call(
        functools.partial(both_kernel, sizes),
        [jax.ShapeDtypeStruct((row_count, hidden), bf16)] + halves,
        (*up_weight, down_weight[back_order[0]], slope, *gathered),
        [pltpu.VMEM((expert_count, splits, row_count, features), bf16)],
        flops=(expert_count + 1) * half,
        vmem=6,
    )
    for turn in back_order[1:]:
        made[turn] = kernel_call(
            functools.partial(down_kernel, sizes),
            halves,
            (down_weight[turn], pre_grad),
            flops=half,
        )

    landed = []
    for turn in back_order:
        keep, give = made[turn]
        paired = keep.astype(f32) + swap(give, 1).astype(f32)
        summed = paired[0]
        for m in reversed(range(1, group_size // 2)):
            summed = summed + swap(paired[m].astype(bf16), 2 * m).astype(f32)
        back = [(target, source) for source, target in routes[turn]]
        landed.append(lax.ppermute(summed.astype(bf16), BOTH, back))

    return kernel_call(
        functools.partial(finish_kernel, expert_count),
        jax.ShapeDtypeStruct((home_rows, features), bf16),
        (grad_out, picked_tokens, *landed),
        [pltpu.VMEM((PADDED, features), bf16)],
    )


def solution(mesh):
    placed = (P("loop", "tensor"), P("tensor", "loop"), P(), P(), P(None, "loop"), P("loop", None))
    return jax.shard_map(
        shards, mesh=mesh, in_specs=placed, out_specs=P("loop", "tensor"), check_vma=False
    )
```

```python
import functools
import math

import jax
import jax.numpy as jnp
from jax import lax
from jax.experimental import pallas as pl
from jax.experimental.pallas import tpu as pltpu
from jax.sharding import PartitionSpec as P

MOST = 28
PADDED = 32
BOTH = ("loop", "tensor")
VMEM = pl.BlockSpec(memory_space=pltpu.VMEM)
LEFT = pl.BlockSpec(memory_space=pl.ANY)

slope_scale = math.sqrt(2.0 / math.pi)


def gelu_slope(values):
    inner = slope_scale * (values + 0.044715 * values * values * values)
    bent = jnp.tanh(inner)
    return 0.5 * (1.0 + bent) + 0.5 * values * (1.0 - bent * bent) * slope_scale * (
        1.0 + 0.134145 * values * values
    )


def rows_dot(left, right):
    return lax.dot_general(left, right, (((1,), (1,)), ((), ())), preferred_element_type=jnp.float32)


def kernel_call(body, out_shape, operands, scratch=(), flops=0, vmem=4, left=0):
    nbytes = sum(o.size * o.dtype.itemsize for o in operands)
    operands = [
        pltpu.with_memory_space_constraint(o, pltpu.HBM) if at < left else o
        for at, o in enumerate(operands)
    ]
    return pl.pallas_call(
        body,
        out_shape=out_shape,
        in_specs=[LEFT] * left + [VMEM] * (len(operands) - left),
        out_specs=jax.tree.map(lambda _: VMEM, out_shape),
        scratch_shapes=scratch,
        cost_estimate=pl.CostEstimate(flops=flops, bytes_accessed=nbytes, transcendentals=0),
        compiler_params=pltpu.CompilerParams(vmem_limit_bytes=vmem << 20),
    )(*operands)


def after_all(values, others):
    values = tuple(values)
    return lax.optimization_barrier((values, tuple(others)))[0]


def swap(values, distance):
    pairs = [(source, source ^ distance) for source in range(lax.axis_size("loop"))]
    return lax.ppermute(values, "loop", pairs)


def home_routes(expert_count):
    loop_size, tensor_size = lax.axis_size("loop"), lax.axis_size("tensor")
    blocks = loop_size // tensor_size
    group_size = loop_size // expert_count
    splits = group_size // blocks
    mirror = blocks // 2 if splits == 1 else 0
    routes = []
    for turn in range(expert_count):
        pairs = []
        for loop_at in range(loop_size):
            for tensor_at in range(tensor_size):
                expert = (tensor_at + turn) % expert_count
                place = (loop_at % blocks) * splits + tensor_at // expert_count
                place ^= mirror if expert != loop_at // blocks else 0
                target = (expert * group_size + place) * tensor_size + loop_at // blocks
                pairs.append((loop_at * tensor_size + tensor_at, target))
        routes.append(pairs)
    return routes


def home_slots(picks, start, home_rows):
    capacity = picks.shape[1]
    first = jnp.sum((picks < start).astype(jnp.int32), axis=1, keepdims=True)
    slot = lax.broadcasted_iota(jnp.int32, (PADDED, capacity), 0)
    listed = lax.broadcasted_iota(jnp.int32, (PADDED, capacity), 1) == first + slot
    local = jnp.sum(jnp.where(listed, picks - start + 1, 0), axis=1, keepdims=True) - 1
    tokens = lax.broadcasted_iota(jnp.int32, (PADDED, home_rows), 1)
    return listed, (tokens == local).astype(jnp.bfloat16)


def prepare_kernel(grad_from, picked_from, gates_from, saved_from, *refs):
    outs, edge, (grad, picked, gates, arrived) = refs[:-5], refs[-5], refs[-4:]
    expert_count = len(outs)
    spare = saved_from.shape[0] - edge.shape[0]
    first = jnp.where(lax.axis_index("tensor") == 0, spare, 0)
    saved_rows = saved_from.at[pl.ds(pl.multiple_of(first, 16), edge.shape[0]), :]
    copies = [
        pltpu.make_async_copy(source, target, arrived.at[at])
        for at, (source, target) in enumerate(
            ((picked_from, picked), (gates_from, gates), (grad_from, grad), (saved_rows, edge))
        )
    ]
    for copy in copies:
        copy.start()
    home_rows = grad.shape[0]
    start = lax.axis_index("loop") * home_rows
    copies[0].wait()
    copies[1].wait()
    rows = []
    for turn in range(expert_count):
        expert = lax.rem(lax.axis_index("tensor") + turn, expert_count)
        listed, chosen = home_slots(picked[pl.ds(expert, 1), :], start, home_rows)
        gate = jnp.sum(jnp.where(listed, gates[pl.ds(expert, 1), :], 0.0), axis=1, keepdims=True)
        rows.append((gate, chosen))
    copies[2].wait()
    for (gate, chosen), out in zip(rows, outs):
        taken = jnp.dot(chosen, grad[...], preferred_element_type=jnp.float32)
        out[...] = (gate * taken).astype(jnp.bfloat16)[:MOST]
    copies[3].wait()


def finish_kernel(blocks, grad, picked, *refs):
    landed, out, held = refs[:-2], refs[-2], refs[-1]
    expert_count = len(landed)
    home_rows = grad.shape[0]
    start = lax.axis_index("loop") * home_rows
    direct = lax.axis_size("tensor") != expert_count
    half = lax.axis_index("loop") // blocks
    total = grad[...].astype(jnp.float32)
    for turn in range(expert_count):
        if direct:
            expert = lax.rem(lax.axis_index("tensor") + turn, expert_count)
        else:
            expert = lax.rem(half - turn + expert_count, expert_count)
        _, chosen = home_slots(picked[pl.ds(expert, 1), :], start, home_rows)
        held[...] = jnp.zeros_like(held)
        held[:MOST, :] = landed[turn][...]
        total += lax.dot_general(
            chosen, held[...], (((0,), (0,)), ((), ())), preferred_element_type=jnp.float32
        )
    out[...] = total.astype(jnp.bfloat16)


def part_start(turn, axis, split, splits, expert_count, group_size, features):
    loop_index = lax.axis_index("loop")
    mine = lax.rem(lax.rem(loop_index, group_size), splits) ^ split
    if axis == 0 and splits == 1:
        share = lax.rem(lax.axis_index("tensor") + turn, expert_count)
    else:
        share = lax.rem(loop_index // group_size - turn + expert_count, expert_count)
    return pl.multiple_of((mine * expert_count + share) * features, 128)


def weight_copies(turn, sizes, axis, weight, out, arrived):
    _, splits, expert_count, group_size = sizes
    features = out.shape[1 + axis]
    parts = arrived.shape[1]
    step = out.shape[1] // parts
    copies = []
    for split in range(splits):
        start = part_start(turn, axis, split, splits, expert_count, group_size, features)
        for at in range(parts):
            rows = pl.ds(at * step, step)
            if axis == 1:
                source = weight.at[rows, pl.ds(start, features)]
            else:
                source = weight.at[pl.ds(pl.multiple_of(start + at * step, 16), step), :]
            copies.append(pltpu.make_async_copy(source, out.at[split, rows], arrived.at[split, at]))
            copies[-1].start()
    return copies


def fetch_kernel(turns, axis, sizes, weight, *refs):
    outs, arrived = refs[:-1], refs[-1]
    copies = []
    for at, turn in enumerate(turns):
        copies += weight_copies(turn, sizes, axis, weight, outs[at], arrived.at[at])
    for copy in copies:
        copy.wait()


def slope_kernel(sizes, home_rows, halo, picked, *refs):
    blocks, splits, _, group_size = sizes
    parts, out = refs[:-1], refs[-1]
    loop_index, tensor_index = lax.axis_index("loop"), lax.axis_index("tensor")
    picks = picked[pl.ds(loop_index // group_size, 1), :]
    place = lax.rem(loop_index, group_size) // splits
    if splits == 1:
        place = jnp.where(loop_index // group_size != tensor_index, place ^ (blocks // 2), place)
    per_tensor = parts[len(parts) // 2].shape[0]
    window = jnp.concatenate([part[...] for part in parts], axis=0)
    for at in range(blocks):
        block = tensor_index * blocks + (place ^ at)
        first = jnp.sum((picks < block * home_rows).astype(jnp.int32), axis=1, keepdims=True)
        wanted = first + lax.broadcasted_iota(jnp.int32, (MOST, window.shape[0]), 0)
        wanted = wanted - tensor_index * per_tensor + halo
        held = lax.broadcasted_iota(jnp.int32, (MOST, window.shape[0]), 1)
        hidden = jnp.dot(
            (held == wanted).astype(jnp.bfloat16), window, preferred_element_type=jnp.float32
        )
        out[at * MOST : (at + 1) * MOST, :] = gelu_slope(hidden)


def join_kernel(*refs):
    for at, part in enumerate(refs[:-1]):
        refs[-1][at] = part[...]


def up_product(sizes, slope, weights, pieces, gathered, pre_grad):
    blocks, splits = sizes[:2]
    hidden = slope.shape[1]
    step = min(512, hidden)
    for turn in range(len(weights)):
        for split in range(splits):
            for at in range(blocks):
                rows = slice(at * MOST, (at + 1) * MOST)
                gathered[turn, split, rows, :] = pieces[at * splits + split][turn]
    for low in range(0, hidden, step):
        columns = slice(low, low + step)
        total = 0.0
        for turn, weight in enumerate(weights):
            for split in range(splits):
                total += rows_dot(gathered[turn, split], weight[split, columns])
        pre_grad[:, columns] = (total * slope[:, columns]).astype(jnp.bfloat16)


def down_product(sizes, pre_grad, weight, keep, give):
    blocks, splits = sizes[:2]
    features = weight.shape[1]
    step = min(512, features)
    for split in range(splits):
        for low in range(0, features, step):
            columns = slice(low, low + step)
            product = rows_dot(pre_grad[...], weight[split, columns]).astype(jnp.bfloat16)
            for at in range(blocks):
                index = at * splits + split
                target = give if index % 2 else keep
                target[index // 2, :, columns] = product[at * MOST : (at + 1) * MOST]


def both_kernel(sizes, *refs):
    expert_count = sizes[2]
    weights, down_weight, slope = refs[:expert_count], refs[expert_count], refs[expert_count + 1]
    pieces, (pre_grad, keep, give, gathered) = refs[expert_count + 2 : -4], refs[-4:]
    up_product(sizes, slope, weights, pieces, gathered, pre_grad)
    down_product(sizes, pre_grad, down_weight, keep, give)


def down_kernel(sizes, weight, pre_grad, keep, give):
    down_product(sizes, pre_grad, weight, keep, give)


def shards(grad_out, saved_hidden, picked_tokens, gate_values, in_weight, out_weight):
    home_rows, features = grad_out.shape
    width, hidden = in_weight.shape
    loop_size, tensor_size = lax.axis_size("loop"), lax.axis_size("tensor")
    expert_count, capacity = picked_tokens.shape
    blocks = loop_size // tensor_size
    group_size = loop_size // expert_count
    splits = group_size // blocks
    sizes = (blocks, splits, expert_count, group_size)
    row_count = blocks * MOST
    routes = home_routes(expert_count)
    bf16, f32 = jnp.bfloat16, jnp.float32

    order = list(range(expert_count))[::-1]
    back_order = order if splits == 1 else order[::-1]
    per_tensor = capacity // tensor_size
    halo = max(
        (
            max(MOST * cut * blocks - cut * per_tensor, cut * per_tensor - capacity + MOST * (tensor_size - cut) * blocks)
            for cut in range(1, tensor_size)
        ),
        default=0,
    )
    halo = -(-halo // 16) * 16
    *outgoing, edge = kernel_call(
        prepare_kernel,
        [jax.ShapeDtypeStruct((MOST, features), bf16)] * expert_count
        + [jax.ShapeDtypeStruct((min(halo, per_tensor // 16 * 16), hidden), bf16)],
        (grad_out, picked_tokens, gate_values, saved_hidden),
        [
            pltpu.VMEM(grad_out.shape, bf16),
            pltpu.VMEM(picked_tokens.shape, jnp.int32),
            pltpu.VMEM(gate_values.shape, f32),
            pltpu.SemaphoreType.DMA((4,)),
        ],
        left=4,
    )
    arrived = {turn: lax.ppermute(outgoing[turn], BOTH, routes[turn]) for turn in order}

    def fetched(turns, axis, weight):
        shape = (splits, hidden, features) if axis == 1 else (splits, features, hidden)
        return kernel_call(
            functools.partial(fetch_kernel, turns, axis, sizes),
            [pltpu.VMEM(shape, bf16)] * expert_count,
            (weight,),
            [pltpu.SemaphoreType.DMA((expert_count, splits, 4))],
            left=1,
        )

    up_weight = fetched(order, 1, *after_all((out_weight,), outgoing))
    arrived = after_all([arrived[turn] for turn in order], up_weight)

    mine = kernel_call(join_kernel, jax.ShapeDtypeStruct((expert_count, MOST, features), bf16), arrived)
    cross = [swap(mine, 2 * m) for m in range(1, group_size // 2)]
    beside = swap(mine, 1)

    saved, edge, down_source = after_all((saved_hidden, edge, in_weight), [beside])
    before, after = [], []
    if tensor_size == 2 and halo <= per_tensor:
        before = after = [lax.ppermute(edge, "tensor", [(0, 1), (1, 0)])]
    else:
        for hop in range(1, -(-halo // per_tensor) + 1):
            part = min(per_tensor, halo - (hop - 1) * per_tensor)
            up = [(at, at + hop) for at in range(tensor_size - hop)]
            before.insert(0, lax.ppermute(saved[per_tensor - part :], "tensor", up))
            after.append(lax.ppermute(saved[:part], "tensor", [(b, a) for a, b in up]))
    slope = kernel_call(
        functools.partial(slope_kernel, sizes, home_rows, halo),
        jax.ShapeDtypeStruct((row_count, hidden), f32),
        (picked_tokens, *before, saved, *after),
        flops=2 * row_count * hidden * (per_tensor + 2 * halo),
    )
    down_weight = fetched(back_order, 0, down_source)
    cross = after_all(cross, [slope, *down_weight])
    down_weight = dict(zip(back_order, down_weight))
    gathered = [mine, beside]
    gathered += [piece for got in cross for piece in (got, swap(got, 1))]

    half = 2 * row_count * hidden * features * splits
    halves = [jax.ShapeDtypeStruct((group_size // 2, MOST, features), bf16)] * 2
    made = {}
    pre_grad, *made[back_order[0]] = kernel_call(
        functools.partial(both_kernel, sizes),
        [jax.ShapeDtypeStruct((row_count, hidden), bf16)] + halves,
        (*up_weight, down_weight[back_order[0]], slope, *gathered),
        [pltpu.VMEM((expert_count, splits, row_count, features), bf16)],
        flops=(expert_count + 1) * half,
        vmem=6,
    )
    for turn in back_order[1:]:
        made[turn] = kernel_call(
            functools.partial(down_kernel, sizes),
            halves,
            (down_weight[turn], pre_grad),
            flops=half,
        )

    totals = {}
    for turn in back_order:
        keep, give = made[turn]
        paired = keep.astype(f32) + swap(give, 1).astype(f32)
        summed = paired[0]
        for m in range(1, group_size // 2):
            summed = summed + swap(paired[m].astype(bf16), 2 * m).astype(f32)
        totals[turn] = summed.astype(bf16)
        if splits == 1 and turn:
            pairs = [(at, (at + turn) % tensor_size) for at in range(tensor_size)]
            totals[turn] = lax.ppermute(totals[turn], "tensor", pairs)

    if splits == 1:
        expert_id, tensor_index = lax.axis_index("loop") // group_size, lax.axis_index("tensor")
        landed = []
        for turn in range(expert_count):
            half_at = (expert_id + turn) % expert_count
            sending = totals[0]
            for other in range(1, expert_count):
                sending = jnp.where((tensor_index - half_at) % tensor_size == other, totals[other], sending)
            pairs = [
                (at, (at // group_size + turn) % expert_count * group_size + (at % group_size ^ (blocks // 2)))
                for at in range(loop_size)
            ]
            landed.append(lax.ppermute(sending, "loop", pairs) if turn else sending)
    else:
        landed = [
            lax.ppermute(totals[turn], BOTH, [(target, source) for source, target in routes[turn]])
            for turn in range(expert_count)
        ]

    return kernel_call(
        functools.partial(finish_kernel, blocks),
        jax.ShapeDtypeStruct((home_rows, features), bf16),
        (grad_out, picked_tokens, *landed),
        [pltpu.VMEM((PADDED, features), bf16)],
    )


def solution(mesh):
    placed = (P("loop", "tensor"), P("tensor", "loop"), P(), P(), P(None, "loop"), P("loop", None))
    return jax.shard_map(
        shards, mesh=mesh, in_specs=placed, out_specs=P("loop", "tensor"), check_vma=False
    )
```

```python
import functools
import math

import jax
import jax.numpy as jnp
from jax import lax
from jax.experimental import pallas as pl
from jax.experimental.pallas import tpu as pltpu
from jax.sharding import PartitionSpec as P

MOST = 28
PADDED = 32
BOTH = ("loop", "tensor")
VMEM = pl.BlockSpec(memory_space=pltpu.VMEM)
LEFT = pl.BlockSpec(memory_space=pl.ANY)

slope_scale = math.sqrt(2.0 / math.pi)


def gelu_slope(values):
    inner = slope_scale * (values + 0.044715 * values * values * values)
    bent = jnp.tanh(inner)
    return 0.5 * (1.0 + bent) + 0.5 * values * (1.0 - bent * bent) * slope_scale * (
        1.0 + 0.134145 * values * values
    )


def rows_dot(left, right):
    return lax.dot_general(left, right, (((1,), (1,)), ((), ())), preferred_element_type=jnp.float32)


def kernel_call(body, out_shape, operands, scratch=(), flops=0, vmem=4, left=0):
    nbytes = sum(o.size * o.dtype.itemsize for o in operands)
    operands = [
        pltpu.with_memory_space_constraint(o, pltpu.HBM) if at < left else o
        for at, o in enumerate(operands)
    ]
    return pl.pallas_call(
        body,
        out_shape=out_shape,
        in_specs=[LEFT] * left + [VMEM] * (len(operands) - left),
        out_specs=jax.tree.map(lambda _: VMEM, out_shape),
        scratch_shapes=scratch,
        cost_estimate=pl.CostEstimate(flops=flops, bytes_accessed=nbytes, transcendentals=0),
        compiler_params=pltpu.CompilerParams(vmem_limit_bytes=vmem << 20),
    )(*operands)


def after_all(values, others):
    values = tuple(values)
    return lax.optimization_barrier((values, tuple(others)))[0]


def swap(values, distance):
    pairs = [(source, source ^ distance) for source in range(lax.axis_size("loop"))]
    return lax.ppermute(values, "loop", pairs)


def home_routes(expert_count):
    loop_size, tensor_size = lax.axis_size("loop"), lax.axis_size("tensor")
    blocks = loop_size // tensor_size
    group_size = loop_size // expert_count
    splits = group_size // blocks
    mirror = blocks // 2 if splits == 1 else 0
    routes = []
    for turn in range(expert_count):
        pairs = []
        for loop_at in range(loop_size):
            for tensor_at in range(tensor_size):
                expert = (tensor_at + turn) % expert_count
                place = (loop_at % blocks) * splits + tensor_at // expert_count
                place ^= mirror if expert != loop_at // blocks else 0
                target = (expert * group_size + place) * tensor_size + loop_at // blocks
                pairs.append((loop_at * tensor_size + tensor_at, target))
        routes.append(pairs)
    return routes


def home_slots(picks, start, home_rows):
    capacity = picks.shape[1]
    first = jnp.sum((picks < start).astype(jnp.int32), axis=1, keepdims=True)
    slot = lax.broadcasted_iota(jnp.int32, (PADDED, capacity), 0)
    listed = lax.broadcasted_iota(jnp.int32, (PADDED, capacity), 1) == first + slot
    local = jnp.sum(jnp.where(listed, picks - start + 1, 0), axis=1, keepdims=True) - 1
    tokens = lax.broadcasted_iota(jnp.int32, (PADDED, home_rows), 1)
    return listed, (tokens == local).astype(jnp.bfloat16)


def prepare_kernel(grad_from, picked_from, gates_from, saved_from, *refs):
    outs, edge, (grad, picked, gates, arrived) = refs[:-5], refs[-5], refs[-4:]
    expert_count = len(outs)
    spare = saved_from.shape[0] - edge.shape[0]
    first = jnp.where(lax.axis_index("tensor") == 0, spare, 0)
    saved_rows = saved_from.at[pl.ds(pl.multiple_of(first, 16), edge.shape[0]), :]
    copies = [
        pltpu.make_async_copy(source, target, arrived.at[at])
        for at, (source, target) in enumerate(
            ((picked_from, picked), (gates_from, gates), (grad_from, grad), (saved_rows, edge))
        )
    ]
    for copy in copies:
        copy.start()
    home_rows = grad.shape[0]
    start = lax.axis_index("loop") * home_rows
    copies[0].wait()
    copies[1].wait()
    rows = []
    for turn in range(expert_count):
        expert = lax.rem(lax.axis_index("tensor") + turn, expert_count)
        listed, chosen = home_slots(picked[pl.ds(expert, 1), :], start, home_rows)
        gate = jnp.sum(jnp.where(listed, gates[pl.ds(expert, 1), :], 0.0), axis=1, keepdims=True)
        rows.append((gate, chosen))
    copies[2].wait()
    for (gate, chosen), out in zip(rows, outs):
        taken = jnp.dot(chosen, grad[...], preferred_element_type=jnp.float32)
        out[...] = (gate * taken).astype(jnp.bfloat16)[:MOST]
    copies[3].wait()


def finish_kernel(blocks, grad, picked, *refs):
    landed, out, held = refs[:-2], refs[-2], refs[-1]
    expert_count = len(landed)
    home_rows = grad.shape[0]
    start = lax.axis_index("loop") * home_rows
    direct = lax.axis_size("tensor") != expert_count
    half = lax.axis_index("loop") // blocks
    total = grad[...].astype(jnp.float32)
    for turn in range(expert_count):
        if direct:
            expert = lax.rem(lax.axis_index("tensor") + turn, expert_count)
        else:
            expert = lax.rem(half - turn + expert_count, expert_count)
        _, chosen = home_slots(picked[pl.ds(expert, 1), :], start, home_rows)
        held[...] = jnp.zeros_like(held)
        held[:MOST, :] = landed[turn][...]
        total += lax.dot_general(
            chosen, held[...], (((0,), (0,)), ((), ())), preferred_element_type=jnp.float32
        )
    out[...] = total.astype(jnp.bfloat16)


def part_start(turn, axis, split, splits, expert_count, group_size, features):
    loop_index = lax.axis_index("loop")
    mine = lax.rem(lax.rem(loop_index, group_size), splits) ^ split
    if axis == 0 and splits == 1:
        share = lax.rem(lax.axis_index("tensor") + turn, expert_count)
    else:
        share = lax.rem(loop_index // group_size - turn + expert_count, expert_count)
    return pl.multiple_of((mine * expert_count + share) * features, 128)


def weight_copies(turn, sizes, axis, weight, out, arrived):
    _, splits, expert_count, group_size = sizes
    features = out.shape[1 + axis]
    parts = arrived.shape[1]
    step = out.shape[1] // parts
    copies = []
    for split in range(splits):
        start = part_start(turn, axis, split, splits, expert_count, group_size, features)
        for at in range(parts):
            rows = pl.ds(at * step, step)
            if axis == 1:
                source = weight.at[rows, pl.ds(start, features)]
            else:
                source = weight.at[pl.ds(pl.multiple_of(start + at * step, 16), step), :]
            copies.append(pltpu.make_async_copy(source, out.at[split, rows], arrived.at[split, at]))
            copies[-1].start()
    return copies


def fetch_kernel(turns, axis, sizes, weight, *refs):
    outs, arrived = refs[:-1], refs[-1]
    copies = []
    for at, turn in enumerate(turns):
        copies += weight_copies(turn, sizes, axis, weight, outs[at], arrived.at[at])
    for copy in copies:
        copy.wait()


def slope_kernel(sizes, home_rows, halo, picked, *refs):
    blocks, splits, _, group_size = sizes
    parts, out = refs[:-1], refs[-1]
    loop_index, tensor_index = lax.axis_index("loop"), lax.axis_index("tensor")
    picks = picked[pl.ds(loop_index // group_size, 1), :]
    place = lax.rem(loop_index, group_size) // splits
    if splits == 1:
        place = jnp.where(loop_index // group_size != tensor_index, place ^ (blocks // 2), place)
    per_tensor = parts[len(parts) // 2].shape[0]
    window = jnp.concatenate([part[...] for part in parts], axis=0)
    for at in range(blocks):
        block = tensor_index * blocks + (place ^ at)
        first = jnp.sum((picks < block * home_rows).astype(jnp.int32), axis=1, keepdims=True)
        wanted = first + lax.broadcasted_iota(jnp.int32, (MOST, window.shape[0]), 0)
        wanted = wanted - tensor_index * per_tensor + halo
        held = lax.broadcasted_iota(jnp.int32, (MOST, window.shape[0]), 1)
        hidden = jnp.dot(
            (held == wanted).astype(jnp.bfloat16), window, preferred_element_type=jnp.float32
        )
        out[at * MOST : (at + 1) * MOST, :] = gelu_slope(hidden)


def join_kernel(*refs):
    for at, part in enumerate(refs[:-1]):
        refs[-1][at] = part[...]


def up_product(sizes, slope, weights, pieces, gathered, pre_grad):
    blocks, splits = sizes[:2]
    hidden = slope.shape[1]
    step = min(512, hidden)
    for turn in range(len(weights)):
        for split in range(splits):
            for at in range(blocks):
                rows = slice(at * MOST, (at + 1) * MOST)
                gathered[turn, split, rows, :] = pieces[at * splits + split][turn]
    for low in range(0, hidden, step):
        columns = slice(low, low + step)
        total = 0.0
        for turn, weight in enumerate(weights):
            for split in range(splits):
                total += rows_dot(gathered[turn, split], weight[split, columns])
        pre_grad[:, columns] = (total * slope[:, columns]).astype(jnp.bfloat16)


def down_product(sizes, pre_grad, weight, keep, give):
    blocks, splits = sizes[:2]
    features = weight.shape[1]
    step = min(512, features)
    for split in range(splits):
        for low in range(0, features, step):
            columns = slice(low, low + step)
            product = rows_dot(pre_grad[...], weight[split, columns]).astype(jnp.bfloat16)
            for at in range(blocks):
                index = at * splits + split
                target = give if index % 2 else keep
                target[index // 2, :, columns] = product[at * MOST : (at + 1) * MOST]


def both_kernel(sizes, *refs):
    expert_count = sizes[2]
    weights, down_weight, slope = refs[:expert_count], refs[expert_count], refs[expert_count + 1]
    pieces, (pre_grad, keep, give, gathered) = refs[expert_count + 2 : -4], refs[-4:]
    up_product(sizes, slope, weights, pieces, gathered, pre_grad)
    down_product(sizes, pre_grad, down_weight, keep, give)


def down_kernel(sizes, weight, pre_grad, keep, give):
    down_product(sizes, pre_grad, weight, keep, give)


def shards(grad_out, saved_hidden, picked_tokens, gate_values, in_weight, out_weight):
    home_rows, features = grad_out.shape
    width, hidden = in_weight.shape
    loop_size, tensor_size = lax.axis_size("loop"), lax.axis_size("tensor")
    expert_count, capacity = picked_tokens.shape
    blocks = loop_size // tensor_size
    group_size = loop_size // expert_count
    splits = group_size // blocks
    sizes = (blocks, splits, expert_count, group_size)
    row_count = blocks * MOST
    routes = home_routes(expert_count)
    bf16, f32 = jnp.bfloat16, jnp.float32

    order = list(range(expert_count))[::-1]
    back_order = order if splits == 1 else order[::-1]
    per_tensor = capacity // tensor_size
    halo = max(
        (
            max(MOST * cut * blocks - cut * per_tensor, cut * per_tensor - capacity + MOST * (tensor_size - cut) * blocks)
            for cut in range(1, tensor_size)
        ),
        default=0,
    )
    halo = -(-halo // 16) * 16
    *outgoing, edge = kernel_call(
        prepare_kernel,
        [jax.ShapeDtypeStruct((MOST, features), bf16)] * expert_count
        + [jax.ShapeDtypeStruct((min(halo, per_tensor // 16 * 16), hidden), bf16)],
        (grad_out, picked_tokens, gate_values, saved_hidden),
        [
            pltpu.VMEM(grad_out.shape, bf16),
            pltpu.VMEM(picked_tokens.shape, jnp.int32),
            pltpu.VMEM(gate_values.shape, f32),
            pltpu.SemaphoreType.DMA((4,)),
        ],
        left=4,
    )
    arrived = {turn: lax.ppermute(outgoing[turn], BOTH, routes[turn]) for turn in order}

    def fetched(turns, axis, weight):
        shape = (splits, hidden, features) if axis == 1 else (splits, features, hidden)
        return kernel_call(
            functools.partial(fetch_kernel, turns, axis, sizes),
            [pltpu.VMEM(shape, bf16)] * expert_count,
            (weight,),
            [pltpu.SemaphoreType.DMA((expert_count, splits, 4))],
            left=1,
        )

    up_weight = fetched(order, 1, *after_all((out_weight,), outgoing))
    arrived = after_all([arrived[turn] for turn in order], up_weight)

    mine = kernel_call(join_kernel, jax.ShapeDtypeStruct((expert_count, MOST, features), bf16), arrived)
    cross = [swap(mine, 2 * m) for m in range(1, group_size // 2)]
    beside = swap(mine, 1)

    saved, edge, down_source = after_all((saved_hidden, edge, in_weight), [beside])
    before, after = [], []
    if tensor_size == 2 and halo <= per_tensor:
        before = after = [lax.ppermute(edge, "tensor", [(0, 1), (1, 0)])]
    else:
        for hop in range(1, -(-halo // per_tensor) + 1):
            part = min(per_tensor, halo - (hop - 1) * per_tensor)
            up = [(at, at + hop) for at in range(tensor_size - hop)]
            before.insert(0, lax.ppermute(saved[per_tensor - part :], "tensor", up))
            after.append(lax.ppermute(saved[:part], "tensor", [(b, a) for a, b in up]))
    slope = kernel_call(
        functools.partial(slope_kernel, sizes, home_rows, halo),
        jax.ShapeDtypeStruct((row_count, hidden), f32),
        (picked_tokens, *before, saved, *after),
        flops=2 * row_count * hidden * (per_tensor + 2 * halo),
    )
    down_weight = fetched(back_order, 0, down_source)
    cross = [after_all((piece,), [slope, *down_weight])[0] for piece in cross]
    down_weight = dict(zip(back_order, down_weight))
    gathered = [mine, beside]
    gathered += [piece for got in cross for piece in (got, swap(got, 1))]

    half = 2 * row_count * hidden * features * splits
    halves = [jax.ShapeDtypeStruct((group_size // 2, MOST, features), bf16)] * 2
    made = {}
    pre_grad, *made[back_order[0]] = kernel_call(
        functools.partial(both_kernel, sizes),
        [jax.ShapeDtypeStruct((row_count, hidden), bf16)] + halves,
        (*up_weight, down_weight[back_order[0]], slope, *gathered),
        [pltpu.VMEM((expert_count, splits, row_count, features), bf16)],
        flops=(expert_count + 1) * half,
        vmem=6,
    )
    for turn in back_order[1:]:
        made[turn] = kernel_call(
            functools.partial(down_kernel, sizes),
            halves,
            (down_weight[turn], pre_grad),
            flops=half,
        )

    totals = {}
    for turn in back_order:
        keep, give = made[turn]
        paired = keep.astype(f32) + swap(give, 1).astype(f32)
        summed = paired[0]
        for m in [group_size // 2 - 1, *range(1, group_size // 2 - 1)]:
            summed = summed + swap(paired[m].astype(bf16), 2 * m).astype(f32)
        totals[turn] = summed.astype(bf16)
        if splits == 1 and turn:
            pairs = [(at, (at + turn) % tensor_size) for at in range(tensor_size)]
            totals[turn] = lax.ppermute(totals[turn], "tensor", pairs)

    if splits == 1:
        expert_id, tensor_index = lax.axis_index("loop") // group_size, lax.axis_index("tensor")
        landed = []
        for turn in range(expert_count):
            half_at = (expert_id + turn) % expert_count
            sending = totals[0]
            for other in range(1, expert_count):
                sending = jnp.where((tensor_index - half_at) % tensor_size == other, totals[other], sending)
            pairs = [
                (at, (at // group_size + turn) % expert_count * group_size + (at % group_size ^ (blocks // 2)))
                for at in range(loop_size)
            ]
            landed.append(lax.ppermute(sending, "loop", pairs) if turn else sending)
    else:
        landed = [
            lax.ppermute(totals[turn], BOTH, [(target, source) for source, target in routes[turn]])
            for turn in range(expert_count)
        ]

    return kernel_call(
        functools.partial(finish_kernel, blocks),
        jax.ShapeDtypeStruct((home_rows, features), bf16),
        (grad_out, picked_tokens, *landed),
        [pltpu.VMEM((PADDED, features), bf16)],
    )


def solution(mesh):
    placed = (P("loop", "tensor"), P("tensor", "loop"), P(), P(), P(None, "loop"), P("loop", None))
    return jax.shard_map(
        shards, mesh=mesh, in_specs=placed, out_specs=P("loop", "tensor"), check_vma=False
    )
```

```python
import functools
import math

import jax
import jax.numpy as jnp
from jax import lax
from jax.experimental import pallas as pl
from jax.experimental.pallas import tpu as pltpu
from jax.sharding import PartitionSpec as P

MOST = 28
PADDED = 32
BOTH = ("loop", "tensor")
VMEM = pl.BlockSpec(memory_space=pltpu.VMEM)
LEFT = pl.BlockSpec(memory_space=pl.ANY)

slope_scale = math.sqrt(2.0 / math.pi)


def gelu_slope(values):
    inner = slope_scale * (values + 0.044715 * values * values * values)
    bent = jnp.tanh(inner)
    return 0.5 * (1.0 + bent) + 0.5 * values * (1.0 - bent * bent) * slope_scale * (
        1.0 + 0.134145 * values * values
    )


def rows_dot(left, right):
    return lax.dot_general(left, right, (((1,), (1,)), ((), ())), preferred_element_type=jnp.float32)


def kernel_call(body, out_shape, operands, scratch=(), flops=0, vmem=4, left=0, out_left=False):
    nbytes = sum(o.size * o.dtype.itemsize for o in operands)
    operands = [
        pltpu.with_memory_space_constraint(o, pltpu.HBM) if at < left else o
        for at, o in enumerate(operands)
    ]
    return pl.pallas_call(
        body,
        out_shape=out_shape,
        in_specs=[LEFT] * left + [VMEM] * (len(operands) - left),
        out_specs=jax.tree.map(lambda _: LEFT if out_left else VMEM, out_shape),
        scratch_shapes=scratch,
        cost_estimate=pl.CostEstimate(flops=flops, bytes_accessed=nbytes, transcendentals=0),
        compiler_params=pltpu.CompilerParams(vmem_limit_bytes=vmem << 20),
    )(*operands)


def after_all(values, others):
    values = tuple(values)
    return lax.optimization_barrier((values, tuple(others)))[0]


def swap(values, distance):
    pairs = [(source, source ^ distance) for source in range(lax.axis_size("loop"))]
    return lax.ppermute(values, "loop", pairs)


def home_routes(expert_count):
    loop_size, tensor_size = lax.axis_size("loop"), lax.axis_size("tensor")
    blocks = loop_size // tensor_size
    group_size = loop_size // expert_count
    splits = group_size // blocks
    mirror = blocks // 2 if splits == 1 else 0
    routes = []
    for turn in range(expert_count):
        pairs = []
        for loop_at in range(loop_size):
            for tensor_at in range(tensor_size):
                expert = (tensor_at + turn) % expert_count
                place = (loop_at % blocks) * splits + tensor_at // expert_count
                place ^= mirror if expert != loop_at // blocks else 0
                target = (expert * group_size + place) * tensor_size + loop_at // blocks
                pairs.append((loop_at * tensor_size + tensor_at, target))
        routes.append(pairs)
    return routes


def home_slots(picks, start, home_rows):
    capacity = picks.shape[1]
    first = jnp.sum((picks < start).astype(jnp.int32), axis=1, keepdims=True)
    slot = lax.broadcasted_iota(jnp.int32, (PADDED, capacity), 0)
    listed = lax.broadcasted_iota(jnp.int32, (PADDED, capacity), 1) == first + slot
    local = jnp.sum(jnp.where(listed, picks - start + 1, 0), axis=1, keepdims=True) - 1
    tokens = lax.broadcasted_iota(jnp.int32, (PADDED, home_rows), 1)
    return listed, (tokens == local).astype(jnp.bfloat16)


def prepare_kernel(grad_from, picked_from, gates_from, saved_from, *refs):
    outs, edge, (grad, picked, gates, arrived) = refs[:-5], refs[-5], refs[-4:]
    expert_count = len(outs)
    spare = saved_from.shape[0] - edge.shape[0]
    first = jnp.where(lax.axis_index("tensor") == 0, spare, 0)
    saved_rows = saved_from.at[pl.ds(pl.multiple_of(first, 16), edge.shape[0]), :]
    copies = [
        pltpu.make_async_copy(source, target, arrived.at[at])
        for at, (source, target) in enumerate(
            ((picked_from, picked), (gates_from, gates), (grad_from, grad), (saved_rows, edge))
        )
    ]
    for copy in copies:
        copy.start()
    home_rows = grad.shape[0]
    start = lax.axis_index("loop") * home_rows
    copies[0].wait()
    copies[1].wait()
    rows = []
    for turn in range(expert_count):
        expert = lax.rem(lax.axis_index("tensor") + turn, expert_count)
        listed, chosen = home_slots(picked[pl.ds(expert, 1), :], start, home_rows)
        gate = jnp.sum(jnp.where(listed, gates[pl.ds(expert, 1), :], 0.0), axis=1, keepdims=True)
        rows.append((gate, chosen))
    copies[2].wait()
    for (gate, chosen), out in zip(rows, outs):
        taken = jnp.dot(chosen, grad[...], preferred_element_type=jnp.float32)
        out[...] = (gate * taken).astype(jnp.bfloat16)[:MOST]
    copies[3].wait()


def landed_expert(turn, blocks, expert_count):
    if lax.axis_size("tensor") != expert_count:
        return lax.rem(lax.axis_index("tensor") + turn, expert_count)
    return lax.rem(lax.axis_index("loop") // blocks - turn + expert_count, expert_count)


def place_rows(chosen, rows, held):
    held[...] = jnp.zeros_like(held)
    held[:MOST, :] = rows[...]
    return lax.dot_general(chosen, held[...], (((0,), (0,)), ((), ())), preferred_element_type=jnp.float32)


def begin_kernel(early, blocks, grad, picked, *refs):
    landed, (total, chosen, held) = refs[:early], refs[early:]
    expert_count = early + chosen.shape[0]
    home_rows = grad.shape[0]
    start = lax.axis_index("loop") * home_rows
    total[...] = grad[...].astype(jnp.float32)
    for turn in range(expert_count):
        expert = landed_expert(turn, blocks, expert_count)
        _, tokens = home_slots(picked[pl.ds(expert, 1), :], start, home_rows)
        if turn < early:
            total[...] += place_rows(tokens, landed[turn], held)
        else:
            chosen[turn - early] = tokens


def finish_kernel(total, chosen, *refs):
    landed, (out, held, ready, sent) = refs[:-4], refs[-4:]
    parts, _, step = ready.shape
    copies = []
    for part in range(parts):
        columns = pl.ds(part * step, step)
        summed = total[:, columns]
        for at, rows in enumerate(landed):
            summed += place_rows(chosen[at], rows.at[:, columns], held)
        ready[part] = summed.astype(jnp.bfloat16)
        copies.append(pltpu.make_async_copy(ready.at[part], out.at[:, columns], sent.at[part]))
        copies[-1].start()
    for copy in copies:
        copy.wait()


def part_start(turn, axis, split, splits, expert_count, group_size, features):
    loop_index = lax.axis_index("loop")
    mine = lax.rem(lax.rem(loop_index, group_size), splits) ^ split
    if axis == 0 and splits == 1:
        share = lax.rem(lax.axis_index("tensor") + turn, expert_count)
    else:
        share = lax.rem(loop_index // group_size - turn + expert_count, expert_count)
    return pl.multiple_of((mine * expert_count + share) * features, 128)


def weight_copies(turn, sizes, axis, weight, out, arrived):
    _, splits, expert_count, group_size = sizes
    features = out.shape[1 + axis]
    parts = arrived.shape[1]
    step = out.shape[1] // parts
    copies = []
    for split in range(splits):
        start = part_start(turn, axis, split, splits, expert_count, group_size, features)
        for at in range(parts):
            rows = pl.ds(at * step, step)
            if axis == 1:
                source = weight.at[rows, pl.ds(start, features)]
            else:
                source = weight.at[pl.ds(pl.multiple_of(start + at * step, 16), step), :]
            copies.append(pltpu.make_async_copy(source, out.at[split, rows], arrived.at[split, at]))
            copies[-1].start()
    return copies


def fetch_kernel(turns, axis, sizes, weight, *refs):
    outs, arrived = refs[:-1], refs[-1]
    copies = []
    for at, turn in enumerate(turns):
        copies += weight_copies(turn, sizes, axis, weight, outs[at], arrived.at[at])
    for copy in copies:
        copy.wait()


def slope_kernel(sizes, home_rows, halo, picked, *refs):
    blocks, splits, _, group_size = sizes
    parts, out = refs[:-1], refs[-1]
    loop_index, tensor_index = lax.axis_index("loop"), lax.axis_index("tensor")
    picks = picked[pl.ds(loop_index // group_size, 1), :]
    place = lax.rem(loop_index, group_size) // splits
    if splits == 1:
        place = jnp.where(loop_index // group_size != tensor_index, place ^ (blocks // 2), place)
    per_tensor = parts[len(parts) // 2].shape[0]
    window = jnp.concatenate([part[...] for part in parts], axis=0)
    for at in range(blocks):
        block = tensor_index * blocks + (place ^ at)
        first = jnp.sum((picks < block * home_rows).astype(jnp.int32), axis=1, keepdims=True)
        wanted = first + lax.broadcasted_iota(jnp.int32, (MOST, window.shape[0]), 0)
        wanted = wanted - tensor_index * per_tensor + halo
        held = lax.broadcasted_iota(jnp.int32, (MOST, window.shape[0]), 1)
        hidden = jnp.dot(
            (held == wanted).astype(jnp.bfloat16), window, preferred_element_type=jnp.float32
        )
        out[at * MOST : (at + 1) * MOST, :] = gelu_slope(hidden)


def join_kernel(*refs):
    for at, part in enumerate(refs[:-1]):
        refs[-1][at] = part[...]


def up_product(sizes, slope, weights, pieces, gathered, pre_grad):
    blocks, splits = sizes[:2]
    hidden = slope.shape[1]
    step = min(512, hidden)
    for turn in range(len(weights)):
        for split in range(splits):
            for at in range(blocks):
                rows = slice(at * MOST, (at + 1) * MOST)
                gathered[turn, split, rows, :] = pieces[at * splits + split][turn]
    for low in range(0, hidden, step):
        columns = slice(low, low + step)
        total = 0.0
        for turn, weight in enumerate(weights):
            for split in range(splits):
                total += rows_dot(gathered[turn, split], weight[split, columns])
        pre_grad[:, columns] = (total * slope[:, columns]).astype(jnp.bfloat16)


def down_product(sizes, pre_grad, weight, keep, give):
    blocks, splits = sizes[:2]
    features = weight.shape[1]
    step = min(512, features)
    for split in range(splits):
        for low in range(0, features, step):
            columns = slice(low, low + step)
            product = rows_dot(pre_grad[...], weight[split, columns]).astype(jnp.bfloat16)
            for at in range(blocks):
                index = at * splits + split
                target = give if index % 2 else keep
                target[index // 2, :, columns] = product[at * MOST : (at + 1) * MOST]


def both_kernel(sizes, *refs):
    expert_count = sizes[2]
    weights, down_weight, slope = refs[:expert_count], refs[expert_count], refs[expert_count + 1]
    pieces, (pre_grad, keep, give, gathered) = refs[expert_count + 2 : -4], refs[-4:]
    up_product(sizes, slope, weights, pieces, gathered, pre_grad)
    down_product(sizes, pre_grad, down_weight, keep, give)


def down_kernel(sizes, weight, pre_grad, keep, give):
    down_product(sizes, pre_grad, weight, keep, give)


def shards(grad_out, saved_hidden, picked_tokens, gate_values, in_weight, out_weight):
    home_rows, features = grad_out.shape
    width, hidden = in_weight.shape
    loop_size, tensor_size = lax.axis_size("loop"), lax.axis_size("tensor")
    expert_count, capacity = picked_tokens.shape
    blocks = loop_size // tensor_size
    group_size = loop_size // expert_count
    splits = group_size // blocks
    sizes = (blocks, splits, expert_count, group_size)
    row_count = blocks * MOST
    routes = home_routes(expert_count)
    bf16, f32 = jnp.bfloat16, jnp.float32

    order = list(range(expert_count))[::-1]
    back_order = order if splits == 1 else order[::-1]
    per_tensor = capacity // tensor_size
    halo = max(
        (
            max(MOST * cut * blocks - cut * per_tensor, cut * per_tensor - capacity + MOST * (tensor_size - cut) * blocks)
            for cut in range(1, tensor_size)
        ),
        default=0,
    )
    halo = -(-halo // 16) * 16
    *outgoing, edge = kernel_call(
        prepare_kernel,
        [jax.ShapeDtypeStruct((MOST, features), bf16)] * expert_count
        + [jax.ShapeDtypeStruct((min(halo, per_tensor // 16 * 16), hidden), bf16)],
        (grad_out, picked_tokens, gate_values, saved_hidden),
        [
            pltpu.VMEM(grad_out.shape, bf16),
            pltpu.VMEM(picked_tokens.shape, jnp.int32),
            pltpu.VMEM(gate_values.shape, f32),
            pltpu.SemaphoreType.DMA((4,)),
        ],
        left=4,
    )
    arrived = {turn: lax.ppermute(outgoing[turn], BOTH, routes[turn]) for turn in order}

    def fetched(turns, axis, weight):
        shape = (splits, hidden, features) if axis == 1 else (splits, features, hidden)
        return kernel_call(
            functools.partial(fetch_kernel, turns, axis, sizes),
            [pltpu.VMEM(shape, bf16)] * expert_count,
            (weight,),
            [pltpu.SemaphoreType.DMA((expert_count, splits, 4))],
            left=1,
        )

    up_weight = fetched(order, 1, *after_all((out_weight,), outgoing))
    arrived = after_all([arrived[turn] for turn in order], up_weight)

    mine = kernel_call(join_kernel, jax.ShapeDtypeStruct((expert_count, MOST, features), bf16), arrived)
    cross = [swap(mine, 2 * m) for m in range(1, group_size // 2)]
    beside = swap(mine, 1)

    saved, edge, down_source = after_all((saved_hidden, edge, in_weight), [beside])
    before, after = [], []
    if tensor_size == 2 and halo <= per_tensor:
        before = after = [lax.ppermute(edge, "tensor", [(0, 1), (1, 0)])]
    else:
        for hop in range(1, -(-halo // per_tensor) + 1):
            part = min(per_tensor, halo - (hop - 1) * per_tensor)
            up = [(at, at + hop) for at in range(tensor_size - hop)]
            before.insert(0, lax.ppermute(saved[per_tensor - part :], "tensor", up))
            after.append(lax.ppermute(saved[:part], "tensor", [(b, a) for a, b in up]))
    slope = kernel_call(
        functools.partial(slope_kernel, sizes, home_rows, halo),
        jax.ShapeDtypeStruct((row_count, hidden), f32),
        (picked_tokens, *before, saved, *after),
        flops=2 * row_count * hidden * (per_tensor + 2 * halo),
    )
    down_weight = fetched(back_order, 0, down_source)
    cross = [after_all((piece,), [slope, *down_weight])[0] for piece in cross]
    down_weight = dict(zip(back_order, down_weight))
    gathered = [mine, beside]
    gathered += [piece for got in cross for piece in (got, swap(got, 1))]

    half = 2 * row_count * hidden * features * splits
    halves = [jax.ShapeDtypeStruct((group_size // 2, MOST, features), bf16)] * 2
    made = {}
    pre_grad, *made[back_order[0]] = kernel_call(
        functools.partial(both_kernel, sizes),
        [jax.ShapeDtypeStruct((row_count, hidden), bf16)] + halves,
        (*up_weight, down_weight[back_order[0]], slope, *gathered),
        [pltpu.VMEM((expert_count, splits, row_count, features), bf16)],
        flops=(expert_count + 1) * half,
        vmem=6,
    )
    for turn in back_order[1:]:
        made[turn] = kernel_call(
            functools.partial(down_kernel, sizes),
            halves,
            (down_weight[turn], pre_grad),
            flops=half,
        )

    totals = {}
    for turn in back_order:
        keep, give = made[turn]
        paired = keep.astype(f32) + swap(give, 1).astype(f32)
        summed = paired[0]
        for m in [group_size // 2 - 1, *range(1, group_size // 2 - 1)]:
            summed = summed + swap(paired[m].astype(bf16), 2 * m).astype(f32)
        totals[turn] = summed.astype(bf16)
        if splits == 1 and turn:
            pairs = [(at, (at + turn) % tensor_size) for at in range(tensor_size)]
            totals[turn] = lax.ppermute(totals[turn], "tensor", pairs)

    if splits == 1:
        expert_id, tensor_index = lax.axis_index("loop") // group_size, lax.axis_index("tensor")
        landed = []
        for turn in range(expert_count):
            half_at = (expert_id + turn) % expert_count
            sending = totals[0]
            for other in range(1, expert_count):
                sending = jnp.where((tensor_index - half_at) % tensor_size == other, totals[other], sending)
            pairs = [
                (at, (at // group_size + turn) % expert_count * group_size + (at % group_size ^ (blocks // 2)))
                for at in range(loop_size)
            ]
            landed.append(lax.ppermute(sending, "loop", pairs) if turn else sending)
    else:
        landed = [
            lax.ppermute(totals[turn], BOTH, [(target, source) for source, target in routes[turn]])
            for turn in range(expert_count)
        ]

    early = 1 if splits == 1 else 0
    begun = kernel_call(
        functools.partial(begin_kernel, early, blocks),
        [
            jax.ShapeDtypeStruct((home_rows, features), f32),
            jax.ShapeDtypeStruct((expert_count - early, PADDED, home_rows), bf16),
        ],
        (grad_out, picked_tokens, *landed[:early]),
        [pltpu.VMEM((PADDED, features), bf16)],
    )
    step = min(512, features)
    return kernel_call(
        finish_kernel,
        pltpu.HBM((home_rows, features), bf16),
        (*begun, *landed[early:]),
        [
            pltpu.VMEM((PADDED, step), bf16),
            pltpu.VMEM((features // step, home_rows, step), bf16),
            pltpu.SemaphoreType.DMA((features // step,)),
        ],
        out_left=True,
    )


def solution(mesh):
    placed = (P("loop", "tensor"), P("tensor", "loop"), P(), P(), P(None, "loop"), P("loop", None))
    return jax.shard_map(
        shards, mesh=mesh, in_specs=placed, out_specs=P("loop", "tensor"), check_vma=False
    )
```

```python
import functools
import math

import jax
import jax.numpy as jnp
from jax import lax
from jax.experimental import pallas as pl
from jax.experimental.pallas import tpu as pltpu
from jax.sharding import PartitionSpec as P

MOST = 28
PADDED = 32
BOTH = ("loop", "tensor")
VMEM = pl.BlockSpec(memory_space=pltpu.VMEM)
LEFT = pl.BlockSpec(memory_space=pl.ANY)

slope_scale = math.sqrt(2.0 / math.pi)


def gelu_slope(values):
    inner = slope_scale * (values + 0.044715 * values * values * values)
    bent = jnp.tanh(inner)
    return 0.5 * (1.0 + bent) + 0.5 * values * (1.0 - bent * bent) * slope_scale * (
        1.0 + 0.134145 * values * values
    )


def rows_dot(left, right):
    return lax.dot_general(left, right, (((1,), (1,)), ((), ())), preferred_element_type=jnp.float32)


def kernel_call(body, out_shape, operands, scratch=(), flops=0, vmem=4, left=0, out_left=False):
    nbytes = sum(o.size * o.dtype.itemsize for o in operands)
    operands = [
        pltpu.with_memory_space_constraint(o, pltpu.HBM) if at < left else o
        for at, o in enumerate(operands)
    ]
    return pl.pallas_call(
        body,
        out_shape=out_shape,
        in_specs=[LEFT] * left + [VMEM] * (len(operands) - left),
        out_specs=jax.tree.map(lambda _: LEFT if out_left else VMEM, out_shape),
        scratch_shapes=scratch,
        cost_estimate=pl.CostEstimate(flops=flops, bytes_accessed=nbytes, transcendentals=0),
        compiler_params=pltpu.CompilerParams(vmem_limit_bytes=vmem << 20),
    )(*operands)


def after_all(values, others):
    values = tuple(values)
    return lax.optimization_barrier((values, tuple(others)))[0]


def swap(values, distance):
    pairs = [(source, source ^ distance) for source in range(lax.axis_size("loop"))]
    return lax.ppermute(values, "loop", pairs)


def home_routes(expert_count):
    loop_size, tensor_size = lax.axis_size("loop"), lax.axis_size("tensor")
    blocks = loop_size // tensor_size
    group_size = loop_size // expert_count
    splits = group_size // blocks
    mirror = blocks // 2 if splits == 1 else 0
    routes = []
    for turn in range(expert_count):
        pairs = []
        for loop_at in range(loop_size):
            for tensor_at in range(tensor_size):
                expert = (tensor_at + turn) % expert_count
                place = (loop_at % blocks) * splits + tensor_at // expert_count
                place ^= mirror if expert != loop_at // blocks else 0
                target = (expert * group_size + place) * tensor_size + loop_at // blocks
                pairs.append((loop_at * tensor_size + tensor_at, target))
        routes.append(pairs)
    return routes


def home_slots(picks, start, home_rows):
    capacity = picks.shape[1]
    first = jnp.sum((picks < start).astype(jnp.int32), axis=1, keepdims=True)
    slot = lax.broadcasted_iota(jnp.int32, (PADDED, capacity), 0)
    listed = lax.broadcasted_iota(jnp.int32, (PADDED, capacity), 1) == first + slot
    local = jnp.sum(jnp.where(listed, picks - start + 1, 0), axis=1, keepdims=True) - 1
    tokens = lax.broadcasted_iota(jnp.int32, (PADDED, home_rows), 1)
    return listed, (tokens == local).astype(jnp.bfloat16)


def prepare_kernel(grad_from, picked_from, gates_from, saved_from, *refs):
    outs, edge, (grad, picked, gates, arrived) = refs[:-5], refs[-5], refs[-4:]
    expert_count = len(outs)
    spare = (saved_from.shape[0] - edge.shape[0]) // 16 * 16
    first = jnp.where(lax.axis_index("tensor") == 0, spare, 0)
    saved_rows = saved_from.at[pl.ds(pl.multiple_of(first, 16), edge.shape[0]), :]
    copies = [
        pltpu.make_async_copy(source, target, arrived.at[at])
        for at, (source, target) in enumerate(
            ((picked_from, picked), (gates_from, gates), (grad_from, grad), (saved_rows, edge))
        )
    ]
    for copy in copies:
        copy.start()
    home_rows = grad.shape[0]
    start = lax.axis_index("loop") * home_rows
    copies[0].wait()
    copies[1].wait()
    rows = []
    for turn in range(expert_count):
        expert = lax.rem(lax.axis_index("tensor") + turn, expert_count)
        listed, chosen = home_slots(picked[pl.ds(expert, 1), :], start, home_rows)
        gate = jnp.sum(jnp.where(listed, gates[pl.ds(expert, 1), :], 0.0), axis=1, keepdims=True)
        rows.append((gate, chosen))
    copies[2].wait()
    for (gate, chosen), out in zip(rows, outs):
        taken = jnp.dot(chosen, grad[...], preferred_element_type=jnp.float32)
        out[...] = (gate * taken).astype(jnp.bfloat16)[:MOST]
    copies[3].wait()


def landed_expert(turn, blocks, expert_count):
    if lax.axis_size("tensor") != expert_count:
        return lax.rem(lax.axis_index("tensor") + turn, expert_count)
    return lax.rem(lax.axis_index("loop") // blocks - turn + expert_count, expert_count)


def place_rows(chosen, rows, held):
    held[...] = jnp.zeros_like(held)
    held[:MOST, :] = rows[...]
    return lax.dot_general(chosen, held[...], (((0,), (0,)), ((), ())), preferred_element_type=jnp.float32)


def begin_kernel(early, blocks, grad, picked, *refs):
    landed, (total, chosen, held) = refs[:early], refs[early:]
    expert_count = early + chosen.shape[0]
    home_rows = grad.shape[0]
    start = lax.axis_index("loop") * home_rows
    total[...] = grad[...].astype(jnp.float32)
    for turn in range(expert_count):
        expert = landed_expert(turn, blocks, expert_count)
        _, tokens = home_slots(picked[pl.ds(expert, 1), :], start, home_rows)
        if turn < early:
            total[...] += place_rows(tokens, landed[turn], held)
        else:
            chosen[turn - early] = tokens


def finish_kernel(total, chosen, *refs):
    landed, (out, held, ready, sent) = refs[:-4], refs[-4:]
    parts, _, step = ready.shape
    copies = []
    for part in range(parts):
        columns = pl.ds(part * step, step)
        summed = total[:, columns]
        for at, rows in enumerate(landed):
            summed += place_rows(chosen[at], rows.at[:, columns], held)
        ready[part] = summed.astype(jnp.bfloat16)
        copies.append(pltpu.make_async_copy(ready.at[part], out.at[:, columns], sent.at[part]))
        copies[-1].start()
    for copy in copies:
        copy.wait()


def part_start(turn, axis, split, splits, expert_count, group_size, features):
    loop_index = lax.axis_index("loop")
    mine = lax.rem(lax.rem(loop_index, group_size), splits) ^ split
    if axis == 0 and splits == 1:
        share = lax.rem(lax.axis_index("tensor") + turn, expert_count)
    else:
        share = lax.rem(loop_index // group_size - turn + expert_count, expert_count)
    return pl.multiple_of((mine * expert_count + share) * features, 128)


def weight_copies(turn, sizes, axis, weight, out, arrived):
    _, splits, expert_count, group_size = sizes
    features = out.shape[1 + axis]
    parts = arrived.shape[1]
    step = out.shape[1] // parts
    copies = []
    for split in range(splits):
        start = part_start(turn, axis, split, splits, expert_count, group_size, features)
        for at in range(parts):
            rows = pl.ds(at * step, step)
            if axis == 1:
                source = weight.at[rows, pl.ds(start, features)]
            else:
                source = weight.at[pl.ds(pl.multiple_of(start + at * step, 16), step), :]
            copies.append(pltpu.make_async_copy(source, out.at[split, rows], arrived.at[split, at]))
            copies[-1].start()
    return copies


def fetch_kernel(turns, axis, sizes, weight, *refs):
    outs, arrived = refs[:-1], refs[-1]
    copies = []
    for at, turn in enumerate(turns):
        copies += weight_copies(turn, sizes, axis, weight, outs[at], arrived.at[at])
    for copy in copies:
        copy.wait()


def slope_kernel(sizes, home_rows, halo, picked, *refs):
    blocks, splits, _, group_size = sizes
    parts, out = refs[:-1], refs[-1]
    loop_index, tensor_index = lax.axis_index("loop"), lax.axis_index("tensor")
    picks = picked[pl.ds(loop_index // group_size, 1), :]
    place = lax.rem(loop_index, group_size) // splits
    if splits == 1:
        place = jnp.where(loop_index // group_size != tensor_index, place ^ (blocks // 2), place)
    per_tensor = parts[len(parts) // 2].shape[0]
    window = jnp.concatenate([part[...] for part in parts], axis=0)
    for at in range(blocks):
        block = tensor_index * blocks + (place ^ at)
        first = jnp.sum((picks < block * home_rows).astype(jnp.int32), axis=1, keepdims=True)
        wanted = first + lax.broadcasted_iota(jnp.int32, (MOST, window.shape[0]), 0)
        wanted = wanted - tensor_index * per_tensor + halo
        held = lax.broadcasted_iota(jnp.int32, (MOST, window.shape[0]), 1)
        hidden = jnp.dot(
            (held == wanted).astype(jnp.bfloat16), window, preferred_element_type=jnp.float32
        )
        out[at * MOST : (at + 1) * MOST, :] = gelu_slope(hidden)


def join_kernel(*refs):
    for at, part in enumerate(refs[:-1]):
        refs[-1][at] = part[...]


def up_product(sizes, slope, weights, pieces, gathered, pre_grad):
    blocks, splits = sizes[:2]
    hidden = slope.shape[1]
    step = min(512, hidden)
    for turn in range(len(weights)):
        for split in range(splits):
            for at in range(blocks):
                rows = slice(at * MOST, (at + 1) * MOST)
                gathered[turn, split, rows, :] = pieces[at * splits + split][turn]
    for low in range(0, hidden, step):
        columns = slice(low, low + step)
        total = 0.0
        for turn, weight in enumerate(weights):
            for split in range(splits):
                total += rows_dot(gathered[turn, split], weight[split, columns])
        pre_grad[:, columns] = (total * slope[:, columns]).astype(jnp.bfloat16)


def down_product(sizes, pre_grad, weight, keep, give):
    blocks, splits = sizes[:2]
    features = weight.shape[1]
    step = min(512, features)
    for split in range(splits):
        for low in range(0, features, step):
            columns = slice(low, low + step)
            product = rows_dot(pre_grad[...], weight[split, columns]).astype(jnp.bfloat16)
            for at in range(blocks):
                index = at * splits + split
                target = give if index % 2 else keep
                target[index // 2, :, columns] = product[at * MOST : (at + 1) * MOST]


def both_kernel(sizes, *refs):
    expert_count = sizes[2]
    weights, down_weight, slope = refs[:expert_count], refs[expert_count], refs[expert_count + 1]
    pieces, (pre_grad, keep, give, gathered) = refs[expert_count + 2 : -4], refs[-4:]
    up_product(sizes, slope, weights, pieces, gathered, pre_grad)
    down_product(sizes, pre_grad, down_weight, keep, give)


def down_kernel(sizes, weight, pre_grad, keep, give):
    down_product(sizes, pre_grad, weight, keep, give)


def shards(grad_out, saved_hidden, picked_tokens, gate_values, in_weight, out_weight):
    home_rows, features = grad_out.shape
    width, hidden = in_weight.shape
    loop_size, tensor_size = lax.axis_size("loop"), lax.axis_size("tensor")
    expert_count, capacity = picked_tokens.shape
    blocks = loop_size // tensor_size
    group_size = loop_size // expert_count
    splits = group_size // blocks
    sizes = (blocks, splits, expert_count, group_size)
    row_count = blocks * MOST
    routes = home_routes(expert_count)
    bf16, f32 = jnp.bfloat16, jnp.float32

    order = list(range(expert_count))[::-1]
    back_order = order if splits == 1 else order[::-1]
    per_tensor = capacity // tensor_size
    halo = max(
        (
            max(MOST * cut * blocks - cut * per_tensor, cut * per_tensor - capacity + MOST * (tensor_size - cut) * blocks)
            for cut in range(1, tensor_size)
        ),
        default=0,
    )
    halo = -(-halo // 16) * 16
    *outgoing, edge = kernel_call(
        prepare_kernel,
        [jax.ShapeDtypeStruct((MOST, features), bf16)] * expert_count
        + [jax.ShapeDtypeStruct((min(halo, per_tensor // 16 * 16), hidden), bf16)],
        (grad_out, picked_tokens, gate_values, saved_hidden),
        [
            pltpu.VMEM(grad_out.shape, bf16),
            pltpu.VMEM(picked_tokens.shape, jnp.int32),
            pltpu.VMEM(gate_values.shape, f32),
            pltpu.SemaphoreType.DMA((4,)),
        ],
        left=4,
    )
    arrived = {turn: lax.ppermute(outgoing[turn], BOTH, routes[turn]) for turn in order}

    def fetched(turns, axis, weight):
        shape = (splits, hidden, features) if axis == 1 else (splits, features, hidden)
        return kernel_call(
            functools.partial(fetch_kernel, turns, axis, sizes),
            [pltpu.VMEM(shape, bf16)] * expert_count,
            (weight,),
            [pltpu.SemaphoreType.DMA((expert_count, splits, 4))],
            left=1,
        )

    up_weight = fetched(order, 1, *after_all((out_weight,), outgoing))
    arrived = after_all([arrived[turn] for turn in order], up_weight)

    mine = kernel_call(join_kernel, jax.ShapeDtypeStruct((expert_count, MOST, features), bf16), arrived)
    cross = [swap(mine, 2 * m) for m in range(1, group_size // 2)]
    beside = swap(mine, 1)

    saved, edge, down_source = after_all((saved_hidden, edge, in_weight), [beside])
    before, after = [], []
    if tensor_size == 2 and halo <= per_tensor and per_tensor % 16 == 0:
        before = after = [lax.ppermute(edge, "tensor", [(0, 1), (1, 0)])]
    else:
        for hop in range(1, -(-halo // per_tensor) + 1):
            part = min(per_tensor, halo - (hop - 1) * per_tensor)
            up = [(at, at + hop) for at in range(tensor_size - hop)]
            before.insert(0, lax.ppermute(saved[per_tensor - part :], "tensor", up))
            after.append(lax.ppermute(saved[:part], "tensor", [(b, a) for a, b in up]))
    slope = kernel_call(
        functools.partial(slope_kernel, sizes, home_rows, halo),
        jax.ShapeDtypeStruct((row_count, hidden), f32),
        (picked_tokens, *before, saved, *after),
        flops=2 * row_count * hidden * (per_tensor + 2 * halo),
    )
    down_weight = fetched(back_order, 0, down_source)
    cross = [after_all((piece,), [slope, *down_weight])[0] for piece in cross]
    down_weight = dict(zip(back_order, down_weight))
    gathered = [mine, beside]
    gathered += [piece for got in cross for piece in (got, swap(got, 1))]

    half = 2 * row_count * hidden * features * splits
    halves = [jax.ShapeDtypeStruct((group_size // 2, MOST, features), bf16)] * 2
    made = {}
    pre_grad, *made[back_order[0]] = kernel_call(
        functools.partial(both_kernel, sizes),
        [jax.ShapeDtypeStruct((row_count, hidden), bf16)] + halves,
        (*up_weight, down_weight[back_order[0]], slope, *gathered),
        [pltpu.VMEM((expert_count, splits, row_count, features), bf16)],
        flops=(expert_count + 1) * half,
        vmem=6,
    )
    for turn in back_order[1:]:
        made[turn] = kernel_call(
            functools.partial(down_kernel, sizes),
            halves,
            (down_weight[turn], pre_grad),
            flops=half,
        )

    totals = {}
    for turn in back_order:
        keep, give = made[turn]
        paired = keep.astype(f32) + swap(give, 1).astype(f32)
        summed = paired[0]
        for m in [group_size // 2 - 1, *range(1, group_size // 2 - 1)]:
            summed = summed + swap(paired[m].astype(bf16), 2 * m).astype(f32)
        totals[turn] = summed.astype(bf16)
        if splits == 1 and turn:
            pairs = [(at, (at + turn) % tensor_size) for at in range(tensor_size)]
            totals[turn] = lax.ppermute(totals[turn], "tensor", pairs)

    if splits == 1:
        expert_id, tensor_index = lax.axis_index("loop") // group_size, lax.axis_index("tensor")
        landed = []
        for turn in range(expert_count):
            half_at = (expert_id + turn) % expert_count
            sending = totals[0]
            for other in range(1, expert_count):
                sending = jnp.where((tensor_index - half_at) % tensor_size == other, totals[other], sending)
            pairs = [
                (at, (at // group_size + turn) % expert_count * group_size + (at % group_size ^ (blocks // 2)))
                for at in range(loop_size)
            ]
            landed.append(lax.ppermute(sending, "loop", pairs) if turn else sending)
    else:
        landed = [
            lax.ppermute(totals[turn], BOTH, [(target, source) for source, target in routes[turn]])
            for turn in range(expert_count)
        ]

    early = 1 if splits == 1 else 0
    begun = kernel_call(
        functools.partial(begin_kernel, early, blocks),
        [
            jax.ShapeDtypeStruct((home_rows, features), f32),
            jax.ShapeDtypeStruct((expert_count - early, PADDED, home_rows), bf16),
        ],
        (grad_out, picked_tokens, *landed[:early]),
        [pltpu.VMEM((PADDED, features), bf16)],
    )
    step = min(512, features)
    return kernel_call(
        finish_kernel,
        pltpu.HBM((home_rows, features), bf16),
        (*begun, *landed[early:]),
        [
            pltpu.VMEM((PADDED, step), bf16),
            pltpu.VMEM((features // step, home_rows, step), bf16),
            pltpu.SemaphoreType.DMA((features // step,)),
        ],
        out_left=True,
    )


def solution(mesh):
    placed = (P("loop", "tensor"), P("tensor", "loop"), P(), P(), P(None, "loop"), P("loop", None))
    return jax.shard_map(
        shards, mesh=mesh, in_specs=placed, out_specs=P("loop", "tensor"), check_vma=False
    )
```

```python
import functools
import math

import jax
import jax.numpy as jnp
from jax import lax
from jax.experimental import pallas as pl
from jax.experimental.pallas import tpu as pltpu
from jax.sharding import PartitionSpec as P

MOST = 28
PADDED = 32
BOTH = ("loop", "tensor")
VMEM = pl.BlockSpec(memory_space=pltpu.VMEM)
LEFT = pl.BlockSpec(memory_space=pl.ANY)

slope_scale = math.sqrt(2.0 / math.pi)


def gelu_slope(values):
    inner = slope_scale * (values + 0.044715 * values * values * values)
    bent = jnp.tanh(inner)
    return 0.5 * (1.0 + bent) + 0.5 * values * (1.0 - bent * bent) * slope_scale * (
        1.0 + 0.134145 * values * values
    )


def rows_dot(left, right):
    return lax.dot_general(left, right, (((1,), (1,)), ((), ())), preferred_element_type=jnp.float32)


def kernel_call(body, out_shape, operands, scratch=(), flops=0, vmem=4, left=0, out_left=False):
    nbytes = sum(o.size * o.dtype.itemsize for o in operands)
    operands = [
        pltpu.with_memory_space_constraint(o, pltpu.HBM) if at < left else o
        for at, o in enumerate(operands)
    ]
    return pl.pallas_call(
        body,
        out_shape=out_shape,
        in_specs=[LEFT] * left + [VMEM] * (len(operands) - left),
        out_specs=jax.tree.map(lambda _: LEFT if out_left else VMEM, out_shape),
        scratch_shapes=scratch,
        cost_estimate=pl.CostEstimate(flops=flops, bytes_accessed=nbytes, transcendentals=0),
        compiler_params=pltpu.CompilerParams(vmem_limit_bytes=vmem << 20),
    )(*operands)


def after_all(values, others):
    values = tuple(values)
    return lax.optimization_barrier((values, tuple(others)))[0]


def swap(values, distance):
    pairs = [(source, source ^ distance) for source in range(lax.axis_size("loop"))]
    return lax.ppermute(values, "loop", pairs)


def home_routes(expert_count):
    loop_size, tensor_size = lax.axis_size("loop"), lax.axis_size("tensor")
    blocks = loop_size // tensor_size
    group_size = loop_size // expert_count
    splits = group_size // blocks
    mirror = blocks // 2 if splits == 1 else 0
    routes = []
    for turn in range(expert_count):
        pairs = []
        for loop_at in range(loop_size):
            for tensor_at in range(tensor_size):
                expert = (tensor_at + turn) % expert_count
                place = (loop_at % blocks) * splits + tensor_at // expert_count
                place ^= mirror if expert != loop_at // blocks else 0
                target = (expert * group_size + place) * tensor_size + loop_at // blocks
                pairs.append((loop_at * tensor_size + tensor_at, target))
        routes.append(pairs)
    return routes


def home_slots(picks, start, home_rows):
    capacity = picks.shape[1]
    first = jnp.sum((picks < start).astype(jnp.int32), axis=1, keepdims=True)
    slot = lax.broadcasted_iota(jnp.int32, (PADDED, capacity), 0)
    listed = lax.broadcasted_iota(jnp.int32, (PADDED, capacity), 1) == first + slot
    local = jnp.sum(jnp.where(listed, picks - start + 1, 0), axis=1, keepdims=True) - 1
    tokens = lax.broadcasted_iota(jnp.int32, (PADDED, home_rows), 1)
    return listed, (tokens == local).astype(jnp.bfloat16)


def prepare_kernel(grad_from, picked_from, gates_from, saved_from, *refs):
    outs, edge, (grad, picked, gates, arrived) = refs[:-5], refs[-5], refs[-4:]
    expert_count = len(outs)
    spare = (saved_from.shape[0] - edge.shape[0]) // 16 * 16
    first = jnp.where(lax.axis_index("tensor") == 0, spare, 0)
    saved_rows = saved_from.at[pl.ds(pl.multiple_of(first, 16), edge.shape[0]), :]
    copies = [
        pltpu.make_async_copy(source, target, arrived.at[at])
        for at, (source, target) in enumerate(
            ((picked_from, picked), (gates_from, gates), (grad_from, grad), (saved_rows, edge))
        )
    ]
    for copy in copies:
        copy.start()
    home_rows = grad.shape[0]
    start = lax.axis_index("loop") * home_rows
    copies[0].wait()
    copies[1].wait()
    rows = []
    for turn in range(expert_count):
        expert = lax.rem(lax.axis_index("tensor") + turn, expert_count)
        listed, chosen = home_slots(picked[pl.ds(expert, 1), :], start, home_rows)
        gate = jnp.sum(jnp.where(listed, gates[pl.ds(expert, 1), :], 0.0), axis=1, keepdims=True)
        rows.append((gate, chosen))
    copies[2].wait()
    for (gate, chosen), out in zip(rows, outs):
        taken = jnp.dot(chosen, grad[...], preferred_element_type=jnp.float32)
        out[...] = (gate * taken).astype(jnp.bfloat16)[:MOST]
    copies[3].wait()


def landed_expert(turn, blocks, expert_count):
    if lax.axis_size("tensor") != expert_count:
        return lax.rem(lax.axis_index("tensor") + turn, expert_count)
    return lax.rem(lax.axis_index("loop") // blocks - turn + expert_count, expert_count)


def place_rows(chosen, rows, held):
    held[:MOST, :] = rows[...]
    return lax.dot_general(chosen, held[...], (((0,), (0,)), ((), ())), preferred_element_type=jnp.float32)


def begin_kernel(early, blocks, grad, picked, *refs):
    landed, (total, chosen, held) = refs[:early], refs[early:]
    expert_count = early + chosen.shape[0]
    home_rows = grad.shape[0]
    start = lax.axis_index("loop") * home_rows
    total[...] = grad[...].astype(jnp.float32)
    held[...] = jnp.zeros_like(held)
    for turn in range(expert_count):
        expert = landed_expert(turn, blocks, expert_count)
        _, tokens = home_slots(picked[pl.ds(expert, 1), :], start, home_rows)
        if turn < early:
            total[...] += place_rows(tokens, landed[turn], held)
        else:
            chosen[turn - early] = tokens


def finish_kernel(total, chosen, *refs):
    landed, (out, held, ready, sent) = refs[:-4], refs[-4:]
    parts, _, step = ready.shape
    held[...] = jnp.zeros_like(held)
    copies = []
    for part in range(parts):
        columns = pl.ds(part * step, step)
        summed = total[:, columns]
        for at, rows in enumerate(landed):
            summed += place_rows(chosen[at], rows.at[:, columns], held)
        ready[part] = summed.astype(jnp.bfloat16)
        copies.append(pltpu.make_async_copy(ready.at[part], out.at[:, columns], sent.at[part]))
        copies[-1].start()
    for copy in copies:
        copy.wait()


def part_start(turn, axis, split, splits, expert_count, group_size, features):
    loop_index = lax.axis_index("loop")
    mine = lax.rem(lax.rem(loop_index, group_size), splits) ^ split
    if axis == 0 and splits == 1:
        share = lax.rem(lax.axis_index("tensor") + turn, expert_count)
    else:
        share = lax.rem(loop_index // group_size - turn + expert_count, expert_count)
    return pl.multiple_of((mine * expert_count + share) * features, 128)


def weight_copies(turn, sizes, axis, weight, out, arrived):
    _, splits, expert_count, group_size = sizes
    features = out.shape[1 + axis]
    parts = arrived.shape[1]
    step = out.shape[1] // parts
    copies = []
    for split in range(splits):
        start = part_start(turn, axis, split, splits, expert_count, group_size, features)
        for at in range(parts):
            rows = pl.ds(at * step, step)
            if axis == 1:
                source = weight.at[rows, pl.ds(start, features)]
            else:
                source = weight.at[pl.ds(pl.multiple_of(start + at * step, 16), step), :]
            copies.append(pltpu.make_async_copy(source, out.at[split, rows], arrived.at[split, at]))
            copies[-1].start()
    return copies


def fetch_kernel(turns, axis, sizes, weight, *refs):
    outs, arrived = refs[:-1], refs[-1]
    copies = []
    for at, turn in enumerate(turns):
        copies += weight_copies(turn, sizes, axis, weight, outs[at], arrived.at[at])
    for copy in copies:
        copy.wait()


def slope_kernel(sizes, home_rows, halo, picked, *refs):
    blocks, splits, _, group_size = sizes
    parts, out = refs[:-1], refs[-1]
    loop_index, tensor_index = lax.axis_index("loop"), lax.axis_index("tensor")
    picks = picked[pl.ds(loop_index // group_size, 1), :]
    place = lax.rem(loop_index, group_size) // splits
    if splits == 1:
        place = jnp.where(loop_index // group_size != tensor_index, place ^ (blocks // 2), place)
    per_tensor = parts[len(parts) // 2].shape[0]
    window = jnp.concatenate([part[...] for part in parts], axis=0)
    for at in range(blocks):
        block = tensor_index * blocks + (place ^ at)
        first = jnp.sum((picks < block * home_rows).astype(jnp.int32), axis=1, keepdims=True)
        wanted = first + lax.broadcasted_iota(jnp.int32, (MOST, window.shape[0]), 0)
        wanted = wanted - tensor_index * per_tensor + halo
        held = lax.broadcasted_iota(jnp.int32, (MOST, window.shape[0]), 1)
        hidden = jnp.dot(
            (held == wanted).astype(jnp.bfloat16), window, preferred_element_type=jnp.float32
        )
        out[at * MOST : (at + 1) * MOST, :] = gelu_slope(hidden)


def join_kernel(*refs):
    for at, part in enumerate(refs[:-1]):
        refs[-1][at] = part[...]


def up_product(sizes, slope, weights, pieces, gathered, pre_grad):
    blocks, splits = sizes[:2]
    hidden = slope.shape[1]
    step = min(256, hidden)
    for turn in range(len(weights)):
        for split in range(splits):
            for at in range(blocks):
                rows = slice(at * MOST, (at + 1) * MOST)
                gathered[turn, split, rows, :] = pieces[at * splits + split][turn]
    for low in range(0, hidden, step):
        columns = slice(low, low + step)
        total = 0.0
        for turn, weight in enumerate(weights):
            for split in range(splits):
                total += rows_dot(gathered[turn, split], weight[split, columns])
        pre_grad[:, columns] = (total * slope[:, columns]).astype(jnp.bfloat16)


def down_product(sizes, pre_grad, weight, keep, give):
    blocks, splits = sizes[:2]
    features = weight.shape[1]
    step = min(512, features)
    for split in range(splits):
        for low in range(0, features, step):
            columns = slice(low, low + step)
            product = rows_dot(pre_grad[...], weight[split, columns]).astype(jnp.bfloat16)
            for at in range(blocks):
                index = at * splits + split
                target = give if index % 2 else keep
                target[index // 2, :, columns] = product[at * MOST : (at + 1) * MOST]


def both_kernel(sizes, *refs):
    expert_count = sizes[2]
    weights, down_weight, slope = refs[:expert_count], refs[expert_count], refs[expert_count + 1]
    pieces, (pre_grad, keep, give, gathered) = refs[expert_count + 2 : -4], refs[-4:]
    up_product(sizes, slope, weights, pieces, gathered, pre_grad)
    down_product(sizes, pre_grad, down_weight, keep, give)


def down_kernel(sizes, weight, pre_grad, keep, give):
    down_product(sizes, pre_grad, weight, keep, give)


def shards(grad_out, saved_hidden, picked_tokens, gate_values, in_weight, out_weight):
    home_rows, features = grad_out.shape
    width, hidden = in_weight.shape
    loop_size, tensor_size = lax.axis_size("loop"), lax.axis_size("tensor")
    expert_count, capacity = picked_tokens.shape
    blocks = loop_size // tensor_size
    group_size = loop_size // expert_count
    splits = group_size // blocks
    sizes = (blocks, splits, expert_count, group_size)
    row_count = blocks * MOST
    routes = home_routes(expert_count)
    bf16, f32 = jnp.bfloat16, jnp.float32

    order = list(range(expert_count))[::-1]
    back_order = order if splits == 1 else order[::-1]
    per_tensor = capacity // tensor_size
    halo = max(
        (
            max(MOST * cut * blocks - cut * per_tensor, cut * per_tensor - capacity + MOST * (tensor_size - cut) * blocks)
            for cut in range(1, tensor_size)
        ),
        default=0,
    )
    halo = -(-halo // 16) * 16
    *outgoing, edge = kernel_call(
        prepare_kernel,
        [jax.ShapeDtypeStruct((MOST, features), bf16)] * expert_count
        + [jax.ShapeDtypeStruct((min(halo, per_tensor // 16 * 16), hidden), bf16)],
        (grad_out, picked_tokens, gate_values, saved_hidden),
        [
            pltpu.VMEM(grad_out.shape, bf16),
            pltpu.VMEM(picked_tokens.shape, jnp.int32),
            pltpu.VMEM(gate_values.shape, f32),
            pltpu.SemaphoreType.DMA((4,)),
        ],
        left=4,
    )
    arrived = {turn: lax.ppermute(outgoing[turn], BOTH, routes[turn]) for turn in order}

    def fetched(turns, axis, weight):
        shape = (splits, hidden, features) if axis == 1 else (splits, features, hidden)
        return kernel_call(
            functools.partial(fetch_kernel, turns, axis, sizes),
            [pltpu.VMEM(shape, bf16)] * expert_count,
            (weight,),
            [pltpu.SemaphoreType.DMA((expert_count, splits, 4))],
            left=1,
        )

    up_weight = fetched(order, 1, *after_all((out_weight,), outgoing))
    arrived = after_all([arrived[turn] for turn in order], up_weight)

    mine = kernel_call(join_kernel, jax.ShapeDtypeStruct((expert_count, MOST, features), bf16), arrived)
    cross = [swap(mine, 2 * m) for m in range(1, group_size // 2)]
    beside = swap(mine, 1)

    saved, edge, down_source = after_all((saved_hidden, edge, in_weight), [beside])
    before, after = [], []
    if tensor_size == 2 and halo <= per_tensor and per_tensor % 16 == 0:
        before = after = [lax.ppermute(edge, "tensor", [(0, 1), (1, 0)])]
    else:
        for hop in range(1, -(-halo // per_tensor) + 1):
            part = min(per_tensor, halo - (hop - 1) * per_tensor)
            up = [(at, at + hop) for at in range(tensor_size - hop)]
            before.insert(0, lax.ppermute(saved[per_tensor - part :], "tensor", up))
            after.append(lax.ppermute(saved[:part], "tensor", [(b, a) for a, b in up]))
    slope = kernel_call(
        functools.partial(slope_kernel, sizes, home_rows, halo),
        jax.ShapeDtypeStruct((row_count, hidden), f32),
        (picked_tokens, *before, saved, *after),
        flops=2 * row_count * hidden * (per_tensor + 2 * halo),
    )
    down_weight = fetched(back_order, 0, down_source)
    cross = [after_all((piece,), [slope, *down_weight])[0] for piece in cross]
    down_weight = dict(zip(back_order, down_weight))
    gathered = [mine, beside]
    gathered += [piece for got in cross for piece in (got, swap(got, 1))]

    half = 2 * row_count * hidden * features * splits
    halves = [jax.ShapeDtypeStruct((group_size // 2, MOST, features), bf16)] * 2
    made = {}
    pre_grad, *made[back_order[0]] = kernel_call(
        functools.partial(both_kernel, sizes),
        [jax.ShapeDtypeStruct((row_count, hidden), bf16)] + halves,
        (*up_weight, down_weight[back_order[0]], slope, *gathered),
        [pltpu.VMEM((expert_count, splits, row_count, features), bf16)],
        flops=(expert_count + 1) * half,
        vmem=6,
    )
    for turn in back_order[1:]:
        made[turn] = kernel_call(
            functools.partial(down_kernel, sizes),
            halves,
            (down_weight[turn], pre_grad),
            flops=half,
        )

    totals = {}
    for turn in back_order:
        keep, give = made[turn]
        paired = keep.astype(f32) + swap(give, 1).astype(f32)
        summed = paired[0]
        for m in [group_size // 2 - 1, *range(1, group_size // 2 - 1)]:
            summed = summed + swap(paired[m].astype(bf16), 2 * m).astype(f32)
        totals[turn] = summed.astype(bf16)
        if splits == 1 and turn:
            pairs = [(at, (at + turn) % tensor_size) for at in range(tensor_size)]
            totals[turn] = lax.ppermute(totals[turn], "tensor", pairs)

    if splits == 1:
        expert_id, tensor_index = lax.axis_index("loop") // group_size, lax.axis_index("tensor")
        landed = []
        for turn in range(expert_count):
            half_at = (expert_id + turn) % expert_count
            sending = totals[0]
            for other in range(1, expert_count):
                sending = jnp.where((tensor_index - half_at) % tensor_size == other, totals[other], sending)
            pairs = [
                (at, (at // group_size + turn) % expert_count * group_size + (at % group_size ^ (blocks // 2)))
                for at in range(loop_size)
            ]
            landed.append(lax.ppermute(sending, "loop", pairs) if turn else sending)
    else:
        landed = [
            lax.ppermute(totals[turn], BOTH, [(target, source) for source, target in routes[turn]])
            for turn in range(expert_count)
        ]

    early = 1 if splits == 1 else 0
    begun = kernel_call(
        functools.partial(begin_kernel, early, blocks),
        [
            jax.ShapeDtypeStruct((home_rows, features), f32),
            jax.ShapeDtypeStruct((expert_count - early, PADDED, home_rows), bf16),
        ],
        (grad_out, picked_tokens, *landed[:early]),
        [pltpu.VMEM((PADDED, features), bf16)],
    )
    step = min(512, features)
    return kernel_call(
        finish_kernel,
        pltpu.HBM((home_rows, features), bf16),
        (*begun, *landed[early:]),
        [
            pltpu.VMEM((PADDED, step), bf16),
            pltpu.VMEM((features // step, home_rows, step), bf16),
            pltpu.SemaphoreType.DMA((features // step,)),
        ],
        out_left=True,
    )


def solution(mesh):
    placed = (P("loop", "tensor"), P("tensor", "loop"), P(), P(), P(None, "loop"), P("loop", None))
    return jax.shard_map(
        shards, mesh=mesh, in_specs=placed, out_specs=P("loop", "tensor"), check_vma=False
    )
```
